128 devices in a mesh: grp: 8 (over x, core), dom: 16 (over z, y).
Axes of the slice: x: 4, y: 4, z: 4, core: 2. Of those that a mesh axis runs over, the one named last changes fastest.
Arguments:
- pattern: int32 [256, 16], replicated, may hold values from 0 to 255, as said below
- density: bfloat16 [256, 16, 128, 128], P(('grp', 'dom')), may hold values from -1 to 1
- hamiltonian: bfloat16 [256, 16, 128, 128], P(('grp', 'dom')), may hold values from -1 to 1
Outputs:
- purified: float32 [256, 16, 128, 128], P(('grp', 'dom'))
- gradient: float32 [256, 16, 128, 128], P(('grp', 'dom'))
The draws below stay inside these ranges and needn't reach their ends.
Inputs may be any that keep to these rules, and one draw needn't show every extreme that they name: `pattern`: slot 0 of block row i is i itself. Slot 1 is a block row of the previous domain group (cyclically) and slot 2 one of the next, each held by the device of the same dom index; the other slots are distinct block rows of the row's own domain group other than i. Block rows are numbered group by group, device by device, 2 to a device.
All inputs are finite; a program needn't handle non-finite values.
Results may differ from the reference program's by a relative error of at most 0.0028.
Values may be sent and summed in bfloat16 or wider, within the bound.
A program may use at most 192 MiB of HBM per device.

```python
import jax
import jax.numpy as jnp
from jax import lax

BLK = 128
NNZ = 16
R_DEV = 2
NB = 256
N_GRP = 8
N_DOM = 16


def draw_pattern(key, part):
    span = NB // N_GRP
    rows_all = jnp.arange(NB, dtype=jnp.int32)

    def one_row(index):
        row_key = jax.random.fold_in(key, index)
        group = index // span
        inner = index % span
        device_index = index // R_DEV % N_DOM
        key_a = jax.random.fold_in(row_key, 1)
        key_b = jax.random.fold_in(row_key, 2)
        key_c = jax.random.fold_in(row_key, 3)
        preceding_rows = jax.random.randint(key_a, (), 0, R_DEV).astype(jnp.int32)
        later_r = jax.random.randint(key_b, (), 0, R_DEV).astype(jnp.int32)
        prior = (group + N_GRP - 1) % N_GRP * span + device_index * R_DEV + preceding_rows
        later = (group + 1) % N_GRP * span + device_index * R_DEV + later_r
        order = jax.random.permutation(key_c, span - 1).astype(jnp.int32)
        picked = order[:NNZ - 3]
        picked = picked + (picked >= inner).astype(jnp.int32)
        picked = group * span + picked
        head = jnp.stack([index, prior, later]).astype(jnp.int32)
        return jnp.concatenate([head, picked.astype(jnp.int32)])
    return jax.vmap(one_row)(rows_all).astype(jnp.int32)


def shard_levels(own_key, shape, pieces, smallest, largest):
    def one(dim, blocks):
        heights = jax.random.uniform(jax.random.fold_in(jax.random.fold_in(own_key, 6), dim), (blocks,), jnp.float32, smallest / len(pieces), largest / len(pieces))
        return jnp.repeat(jnp.exp(heights), shape[dim] // blocks).reshape((-1,) + (1,) * (len(shape) - dim - 1))

    loudness = one(*pieces[0])
    for cut in pieces[1:]:
        loudness = loudness * one(*cut)
    return loudness


def centred(own_key, extent, scale, bound, split=(), held_as=jnp.bfloat16):
    level = shard_levels(own_key, extent, split, -0.22, 0.18) if split else 1.0
    entries = jax.random.normal(own_key, extent, jnp.float32) * scale * level
    return jnp.minimum(jnp.maximum(entries, -bound), bound).astype(held_as)


def setup_inputs(seed: int = 0) -> dict:
    keys = jax.random.split(jax.random.key(seed), 4)
    pattern = draw_pattern(jax.random.fold_in(keys[3], 71), 0)
    density = centred(keys[1], (NB, NNZ, BLK, BLK), 0.15, 1.0, ((0, 128),))
    hamiltonian = centred(keys[2], (NB, NNZ, BLK, BLK), 0.15, 1.0, ((0, 128),))
    return dict(pattern=pattern, density=density, hamiltonian=hamiltonian)


def masked(left_rows, right_rows, pattern):
    def one_row(items):
        block_row_list, cols = items
        chosen = jnp.take(right_rows, cols, axis=0).astype(jnp.float32)
        far_cols = jnp.take(pattern, cols, axis=0)
        match = (far_cols[:, None, :] == cols[None, :, None]).astype(jnp.float32)
        select_blocks = jnp.einsum("tsu,tucb->tscb", match, chosen)
        return jnp.einsum("xgz,xkzq->kgq", block_row_list.astype(jnp.float32), select_blocks)
    return lax.map(one_row, (left_rows, pattern))


def reference(pattern, density, hamiltonian):
    square = masked(density, density, pattern)
    left = masked(density, hamiltonian, pattern)
    right = masked(hamiltonian, density, pattern)
    square_b = square.astype(jnp.bfloat16)
    left_block_rows = left.astype(jnp.bfloat16)
    right_b = right.astype(jnp.bfloat16)
    cube = masked(square_b, density, pattern)
    square_h = masked(square_b, hamiltonian, pattern)
    sandwich = masked(left_block_rows, density, pattern)
    h_square = masked(right_b, density, pattern)
    purified = 3.0 * square - 2.0 * cube
    gradient = 3.0 * (left + right) - 2.0 * (square_h + sandwich + h_square)
    return purified, gradient
```

```python
import functools

import jax
import jax.numpy as jnp
from jax import lax
from jax.experimental import pallas as pl
from jax.experimental.pallas import tpu as pltpu
from jax.sharding import PartitionSpec as P

MESH = pl.DeviceIdType.MESH
BLK = 128
NNZ = 16
KEPT = 14
SPAN = 32
GROUPS = 8
EXTRA = SPAN * KEPT
TOTAL = EXTRA + 4 + 6 + 6
CUT = 6
ZH = CUT // 2
CHUNK = 2
STEP = 8
ENTRIES = NNZ * NNZ
YH = CUT + (KEPT - CUT) // 2
PARTS = ((CUT + 2, NNZ, CUT), (0, 1, 0), (3, CUT + 2, 1))

EVENTS = {
    "Zp": ((0, CUT), 0, 0, "zp"),
    "Zm": ((0, CUT), 0, 0, "zm"),
    "ZpF": ((0, ZH), -1, 0, "zp"),
    "ZmF": ((ZH, CUT), 1, 0, "zm"),
    "ZY0": ((0, CUT), 0, 0, "y"),
    "ZYm": ((0, CUT), -1, 0, "y"),
    "ZYp": ((0, CUT), 1, 0, "y"),
    "ZYa": ((0, ZH), 2, 0, "y"),
    "ZYb": ((ZH, CUT), 2, 0, "y"),
    "Y": ((CUT, KEPT), 0, 0, "y"),
    "Yp": ((CUT, KEPT), 0, 0, "zp"),
    "Ym": ((CUT, KEPT), 0, 0, "zm"),
    "YpF": ((CUT, YH), -1, 0, "zp"),
    "YmF": ((YH, KEPT), 1, 0, "zm"),
    "Xp": ((CUT, KEPT), 0, 1, "zp"),
    "Xm": ((CUT, KEPT), 0, 1, "zm"),
    "XpF": ((CUT, YH), -1, 1, "zp"),
    "XmF": ((YH, KEPT), 1, 1, "zm"),
}
NAMES = tuple(EVENTS)
N_EV = len(NAMES)
ORDER = (
    "R Zp O", "R Zm O", "S ZpF O", "S ZmF O", "R Y O", "S Xp O", "S Xm O", "QY",
    "S Y Q", "S Yp Q", "S Ym Q", "S ZY0 O", "S ZYm O", "S ZYp O", "R Yp O", "R Ym O",
    "S YpF O", "S YmF O", "QZ", "S Zp Q", "S Zm Q", "R Y Q", "S Xp Q", "S Xm Q",
    "R ZpF O", "R ZmF O", "S ZYa O", "S ZYb O", "S ZY0 Q", "R Xp O", "R Xm O", "S XpF O",
    "S XmF O", "R YpF O", "R YmF O", "R ZY0 O", "R Yp Q", "R Ym Q", "S YpF Q", "S YmF Q",
    "R Zp Q", "R Zm Q", "S ZpF Q", "S ZmF Q", "S ZYm Q", "S ZYp Q", "R ZYm O", "R Xp Q",
    "R Xm Q", "S XpF Q", "S XmF Q", "R ZpF Q", "R ZmF Q", "S ZYa Q", "S ZYb Q", "R ZYp O",
    "R XpF O", "R XmF O", "R YpF Q", "R YmF Q", "R ZYa O", "R ZYb O", "R ZY0 Q", "R ZYm Q",
    "R ZYp Q", "R XpF Q", "R XmF Q", "R ZYa Q", "R ZYb Q",
)


def gather_kernel(
    p_ref, h_ref, all_ref,
    ss, rs, ds, dr, loc, ins, inr, qs, qr, es, er, xs, xr,
):
    args = (p_ref, h_ref)
    g, d = lax.axis_index("grp"), lax.axis_index("dom")
    x, c = g // 2, g % 2
    z, y = d // 4, d % 4
    host = y // 2
    yn, yq = y + 1 - 2 * (y % 2), 3 - y
    dq = z * 4 + yq
    sib_g = g + 1 - 2 * c
    sibling = (sib_g, d)
    ways = {
        "zp": (g, (z + 1) % 4 * 4 + y),
        "zm": (g, (z + 3) % 4 * 4 + y),
        "y": (g, z * 4 + yn),
    }
    is_own = (c + host + 1) % 2
    work_g = is_own * g + (1 - is_own) * sib_g
    work_d = is_own * d + (1 - is_own) * dq
    up, down = (g + 1) % GROUPS, (g + GROUPS - 1) % GROUPS
    up_t = (is_own * (up + 1 - 2 * (up % 2)) + (1 - is_own) * up, is_own * dq + (1 - is_own) * d)
    down_t = (is_own * (down + 1 - 2 * (down % 2)) + (1 - is_own) * down, is_own * dq + (1 - is_own) * d)
    partner_idle = (2 * x + host, dq)

    barrier = pltpu.get_barrier_semaphore()
    for who in (
        *ways.values(), sibling, partner_idle,
        ((work_g + GROUPS - 1) % GROUPS, work_d), ((work_g + 1) % GROUPS, work_d),
    ):
        pl.semaphore_signal(barrier, inc=1, device_id=who, device_id_type=MESH)
    pl.semaphore_wait(barrier, 8 - 2 * is_own)

    def at(dom, row, lo, n):
        return all_ref.at[pl.ds((dom * 2 + row) * KEPT + lo, n)]

    def at1(dom, row, lo, n, a):
        return all_ref.at[pl.ds((dom * 2 + row) * KEPT + lo, n), a]

    def remote(src, dst, s, r, who):
        return pltpu.make_async_remote_copy(
            src_ref=src, dst_ref=dst, send_sem=s, recv_sem=r, device_id=who, device_id_type=MESH
        )

    def init_copies(row, to):
        out = []
        for k, (s0, s1, b) in enumerate(PARTS):
            for a in range(2):
                src = args[a].at[row, pl.ds(s0, s1 - s0)]
                dst = at1(d, row, b, s1 - s0, a)
                if to == "own":
                    out.append(pltpu.make_async_copy(src, dst, loc.at[row, k, a]))
                elif to == "sibling":
                    out.append(remote(src, dst, ins.at[row, k, a], inr.at[row, k, a], sibling))
                else:
                    out.append(remote(src, dst, qs.at[row, k, a], qr.at[k, a], (2 * x + row, dq)))
        return out

    def extra_copies(to):
        out = []
        for row in range(2):
            for a in range(2):
                src = args[a].at[row, pl.ds(1, 2)]
                dst = all_ref.at[pl.ds(EXTRA + 2 * row, 2), a]
                if to == "own":
                    out.append(pltpu.make_async_copy(src, dst, es.at[row, a]))
                else:
                    out.append(remote(src, dst, es.at[row, a], er.at[row, a], (sib_g, dq)))
        return out

    def side_copies():
        out = []
        for k, who in enumerate((up_t, down_t)):
            for row in range(2):
                for a in range(2):
                    src = args[a].at[row, pl.ds(0, 3)]
                    dst = all_ref.at[pl.ds(EXTRA + 4 + 6 * k + 3 * row, 3), a]
                    out.append(remote(src, dst, xs.at[k, row, a], xr.at[k, row, a], who))
        return out

    own = c == host
    for core in range(2):

        @pl.when(jnp.logical_and(own, c == core))
        def _():
            mine = init_copies(core, "own")
            theirs = init_copies(1 - core, "sibling")
            for m, t in zip(mine, theirs):
                m.start()
                t.start()
            for copy in init_copies(core, "sibling") + init_copies(1 - core, "own"):
                copy.start()
            for copy in mine:
                copy.wait()

        @pl.when(jnp.logical_and(jnp.logical_not(own), c == core))
        def _():
            for m, t in zip(init_copies(0, "partner"), init_copies(1, "partner")):
                m.start()
                t.start()
            for copy in init_copies(core, "sibling"):
                copy.wait_recv()

    def dom_of(zz, col, kind):
        yy = y if col == 0 else yn
        return (z + zz + 4) % 4 * 4 + (yy if kind == "O" else 3 - yy)

    def event(name, kind, side):
        (lo, hi), zz, col, way = EVENTS[name]
        k = NAMES.index(name) + (N_EV if kind == "Q" else 0)
        if side == "R":
            if way == "zp":
                zz -= 1
            elif way == "zm":
                zz += 1
            else:
                col = 1
        dom = dom_of(zz, col, kind)
        ref = at(dom, c, lo, hi - lo)
        return remote(ref, ref, ss.at[k], rs.at[k], ways[way]), (dom, lo, hi - lo, k)

    passed = []

    def to_sibling(dom, lo, n, k):
        ref = at(dom, c, lo, n)
        remote(ref, ref, ds.at[k], dr.at[k], sibling).start()
        passed.append((dom, lo, n, k))

    sent = []

    def send(name, kind):
        copy, _ = event(name, kind, "S")
        copy.start()
        sent.append(copy)

    def receive(name, kind):
        copy, what = event(name, kind, "R")
        copy.wait_recv()
        to_sibling(*what)

    def receive_partner(parts, lo, n, k):
        for part in parts:
            s0, s1, b = PARTS[part]
            for a in range(2):
                ref = at1(dq, c, b, s1 - s0, a)
                remote(ref, ref, qs.at[0, part, a], qr.at[part, a], sibling).wait_recv()
        to_sibling(dq, lo, n, k)

    for name in ("Y", "Zp", "Zm", "Yp", "Ym"):
        send(name, "O")

    sides = side_copies()
    for copy in sides:
        copy.start()

    @pl.when(own)
    def _():
        for copy in extra_copies("own"):
            copy.start()

    @pl.when(jnp.logical_not(own))
    def _():
        for copy in extra_copies("partner"):
            copy.start()

    for step in ORDER:
        if step == "QY":
            receive_partner((0,), CUT, KEPT - CUT, 2 * N_EV)
        elif step == "QZ":
            receive_partner((1, 2), 0, CUT, 2 * N_EV + 1)
        else:
            what, name, kind = step.split()
            (send if what == "S" else receive)(name, kind)

    for core in range(2):

        @pl.when(jnp.logical_and(own, c == core))
        def _():
            for copy in init_copies(1 - core, "own") + extra_copies("own"):
                copy.wait()
            for copy in init_copies(0, "sibling") + init_copies(1, "sibling"):
                copy.wait_send()

        @pl.when(jnp.logical_and(jnp.logical_not(own), c == core))
        def _():
            for copy in init_copies(1 - core, "sibling"):
                copy.wait_recv()
            for copy in init_copies(0, "partner") + init_copies(1, "partner"):
                copy.wait_send()
            for copy in extra_copies("partner"):
                copy.wait()

    for copy in sides:
        copy.wait()
    for copy in sent:
        copy.wait_send()
    for dom, lo, n, k in passed:
        mine, theirs = at(dom, c, lo, n), at(dom, 1 - c, lo, n)
        remote(mine, mine, ds.at[k], dr.at[k], sibling).wait_send()
        remote(theirs, theirs, ds.at[k], dr.at[k], sibling).wait_recv()


def gather(density, hamiltonian):
    dma = pltpu.SemaphoreType.DMA
    return pl.pallas_call(
        gather_kernel,
        name="gather",
        out_shape=jax.ShapeDtypeStruct((TOTAL, 2, BLK, BLK), jnp.bfloat16),
        in_specs=[pl.BlockSpec(memory_space=pl.ANY)] * 2,
        out_specs=pl.BlockSpec(memory_space=pl.ANY),
        scratch_shapes=[
            dma((2 * N_EV,)), dma((2 * N_EV,)), dma((2 * N_EV + 2,)), dma((2 * N_EV + 2,)),
            dma((2, 3, 2)), dma((2, 3, 2)), dma((2, 3, 2)), dma((2, 3, 2)), dma((3, 2)),
            dma((2, 2)), dma((2, 2)), dma((2, 2, 2)), dma((2, 2, 2)),
        ],
        compiler_params=pltpu.CompilerParams(collective_id=0, has_side_effects=True),
    )(density, hamiltonian)


def row_kernel(
    steps, chunk_s, slots, places, mine, all_ref, x_ref, g_ref, send_ref,
    left, right, low, high, mid, sem_a, sem_b,
):
    def fetch_left(lo, n, at):
        return pltpu.make_async_copy(
            all_ref.at[pl.ds(at, n)], left.at[pl.ds(lo, n)], sem_a.at[lo // KEPT]
        )

    def fetch(e):
        return pltpu.make_async_copy(all_ref.at[places[e]], right.at[e], sem_b.at[e])

    def fetch_step(q, what):
        for k in range(STEP * CHUNK):
            what(fetch(q * (STEP * CHUNK) + k))

    a_copies = (fetch_left(0, KEPT, mine[0]), fetch_left(KEPT, 2, mine[1]))
    for copy in a_copies:
        copy.start()

    @pl.loop(0, steps[0])
    def _(q):
        fetch_step(q, lambda copy: copy.start())

    left[NNZ] = jnp.zeros((2, BLK, BLK), jnp.bfloat16)
    mid[NNZ] = jnp.zeros((2, BLK, BLK), jnp.bfloat16)
    for s in range(NNZ):
        low[s] = jnp.zeros((BLK, 2 * BLK), jnp.float32)
        high[s] = jnp.zeros((BLK, 2 * BLK), jnp.float32)
    for copy in a_copies:
        copy.wait()

    def step(q, a_ref, total):
        sums = []
        for k in range(STEP):
            first = (q * STEP + k) * CHUNK
            e = [first + p for p in range(CHUNK)]
            t = [slots[p] for p in e]
            a = jnp.concatenate([a_ref[p, 0] for p in t], axis=1)
            b = jnp.concatenate([a_ref[p, 1] for p in t], axis=1)
            den = jnp.concatenate([right[p, 0] for p in e], axis=0)
            ham = jnp.concatenate([right[p, 1] for p in e], axis=0)
            both = jnp.dot(a, jnp.concatenate([den, ham], axis=1), preferred_element_type=jnp.float32)
            more = jnp.dot(b, den, preferred_element_type=jnp.float32)
            sums.append((both, more))
        for k in range(STEP):
            s = chunk_s[q * STEP + k]
            both, more = sums[k]
            total[s, :, :BLK] += both[:, :BLK]
            total[s, :, BLK:] += both[:, BLK:] + more

    @pl.loop(0, steps[0])
    def _(q):
        fetch_step(q, lambda copy: copy.wait())
        step(q, left, low)

    for s in range(NNZ):
        at = 0 if s == 0 else KEPT - 1 + s if s < 3 else s - 2
        mid[at, 0] = low[s, :, :BLK].astype(jnp.bfloat16)
        mid[at, 1] = low[s, :, BLK:].astype(jnp.bfloat16)

    @pl.loop(0, steps[0])
    def _(q):
        step(q, mid, high)

    for s in range(NNZ):
        purified = 3.0 * low[s, :, :BLK] - 2.0 * high[s, :, :BLK]
        gradient = 3.0 * low[s, :, BLK:] - 2.0 * high[s, :, BLK:]
        x_ref[s] = purified
        g_ref[s] = gradient
        send_ref[0, s] = purified.astype(jnp.bfloat16)
        send_ref[1, s] = gradient.astype(jnp.bfloat16)


def one_row(name, steps, chunk_s, slots, places, mine, everything):
    f32, bf16 = jnp.float32, jnp.bfloat16
    vmem = pl.BlockSpec(memory_space=pltpu.VMEM)
    smem = pl.BlockSpec(memory_space=pltpu.SMEM)
    return pl.pallas_call(
        row_kernel,
        name=name,
        out_shape=(
            jax.ShapeDtypeStruct((NNZ, BLK, BLK), f32),
            jax.ShapeDtypeStruct((NNZ, BLK, BLK), f32),
            jax.ShapeDtypeStruct((2, NNZ, BLK, BLK), bf16),
        ),
        in_specs=[smem] * 5 + [pl.BlockSpec(memory_space=pl.ANY)],
        out_specs=(vmem, vmem, vmem),
        scratch_shapes=[
            pltpu.VMEM((NNZ + 1, 2, BLK, BLK), bf16),
            pltpu.VMEM((ENTRIES, 2, BLK, BLK), bf16),
            pltpu.VMEM((NNZ + 1, BLK, 2 * BLK), f32),
            pltpu.VMEM((NNZ + 1, BLK, 2 * BLK), f32),
            pltpu.VMEM((NNZ + 1, 2, BLK, BLK), bf16),
            pltpu.SemaphoreType.DMA((2,)),
            pltpu.SemaphoreType.DMA((ENTRIES,)),
        ],
        compiler_params=pltpu.CompilerParams(vmem_limit_bytes=40 << 20),
        cost_estimate=pl.CostEstimate(
            flops=2 * 2 * 3 * 104 * BLK**3, bytes_accessed=14 << 20, transcendentals=0
        ),
    )(steps, chunk_s, slots, places, mine, everything)


def tables(pattern, work_g, work_d):
    first = work_g * SPAN + work_d * 2
    cols = lax.dynamic_slice_in_dim(pattern, first, 2, 0)
    far = jnp.take(pattern, cols, axis=0)
    slot = jnp.arange(NNZ, dtype=jnp.int32)
    found = jnp.max(
        jnp.where(far[:, :, None, :] == cols[:, None, :, None], slot + 1, 0), axis=3
    ) - 1
    group, inner = cols // SPAN, cols % SPAN
    row = cols % 2
    inside = (group == work_g)[:, :, None]
    before = (group == (work_g + GROUPS - 1) % GROUPS)[:, :, None]
    short = jnp.clip(found, 0, 2)
    place = jnp.where(
        inside,
        jnp.where(
            (found == 1) | (found == 2),
            EXTRA + 2 * row[:, :, None] + jnp.clip(found - 1, 0, 1),
            inner[:, :, None] * KEPT + jnp.where(found < 3, 0, found - 2),
        ),
        EXTRA + 4 + 3 * row[:, :, None] + short + jnp.where(before, 0, 6),
    )
    hit = found >= 0
    held = hit.astype(jnp.int32)
    count = jnp.sum(held, axis=1)
    rank = jnp.sum(jnp.where(slot[None, :, None, None] > slot[None, None, :, None], held[:, None], 0), axis=2)
    chunks = (count + CHUNK - 1) // CHUNK
    start = jnp.sum(jnp.where(slot[None, None, :] < slot[None, :, None], chunks[:, None, :], 0), axis=2)
    spot = jnp.where(hit, start[:, None, :] * CHUNK + rank, -1).reshape(2, 1, NNZ * NNZ)
    chosen = spot == jnp.arange(ENTRIES, dtype=jnp.int32)[None, :, None]
    left_at = jnp.where(slot == 0, 0, jnp.where(slot < 3, KEPT - 1 + slot, slot - 2))
    both = jnp.broadcast_to(left_at[None, :, None] - NNZ, found.shape) + place * 32
    both = jnp.sum(jnp.where(chosen, both.reshape(2, 1, NNZ * NNZ) + NNZ, 0), axis=2)
    slots = jnp.where(jnp.any(chosen, axis=2), both % 32, NNZ)
    places = both // 32
    c = jnp.arange(ENTRIES // CHUNK, dtype=jnp.int32)[None, :, None]
    chunk_s = jnp.sum((c >= (start + chunks)[:, None, :]).astype(jnp.int32), axis=2)
    steps = (jnp.sum(chunks, axis=1, keepdims=True) + STEP - 1) // STEP
    return steps, chunk_s, slots, places


def on_device(pattern, density, hamiltonian):
    g, d = lax.axis_index("grp"), lax.axis_index("dom")
    y = d % 4
    own = g % 2 == y // 2
    work_g = jnp.where(own, g, g + 1 - 2 * (g % 2))
    work_d = jnp.where(own, d, d + 3 - 2 * y)
    lists = tables(pattern, work_g, work_d)
    everything = gather(density, hamiltonian)
    pairs = []
    for gg in range(8):
        for dd in range(16):
            yy = dd % 4
            if gg % 2 != yy // 2:
                pairs.append((gg * 16 + dd, (gg ^ 1) * 16 + dd + 3 - 2 * yy))
    mine, back = [], []
    for w in range(2):
        where = jnp.stack([(work_d * 2 + w) * KEPT, jnp.int32(EXTRA + 2 * w)])
        px, gx, out = one_row(f"row{w}", *(v[w] for v in lists), where, everything)
        mine.append((px, gx))
        back.append(lax.ppermute(out, ("grp", "dom"), pairs))
    res = []
    for k in range(2):
        res.append(jnp.stack([
            jnp.where(own, mine[w][k], back[w][k].astype(jnp.float32)) for w in range(2)
        ]))
    return tuple(res)


def solution(mesh):
    split = P(("grp", "dom"), None, None, None)
    return jax.shard_map(
        on_device,
        mesh=mesh,
        in_specs=(P(), split, split),
        out_specs=(split, split),
        check_vma=False,
    )
```

```python
import functools

import jax
import jax.numpy as jnp
from jax import lax
from jax.experimental import pallas as pl
from jax.experimental.pallas import tpu as pltpu
from jax.sharding import PartitionSpec as P

MESH = pl.DeviceIdType.MESH
BLK = 128
NNZ = 16
KEPT = 14
SPAN = 32
GROUPS = 8
EXTRA = SPAN * KEPT
TOTAL = EXTRA + 4 + 6 + 6
CHUNK = 2
STEP = 8
ENTRIES = NNZ * NNZ
CUT = {"O": 5, "Q": 4}
PARTS = ((CUT["Q"] + 2, NNZ, CUT["Q"]), (0, 1, 0), (3, CUT["Q"] + 2, 1))

EVENTS = {
    "SZ": ("Z", "u", "v", "single"),
    "PZ": ("Z", "u", "v", "pair"),
    "FZ": ("Z", "u", "vs", "pair"),
    "C0": ("Z", "u", "v", "cross"),
    "Cs": ("Z", "u", "vs", "cross"),
    "Cp": ("Z", "u", "vp", "cross"),
    "Cf": ("Z", "u", "vf", "cross"),
    "Y": ("Y", "u", "v", "cross"),
    "SY": ("Y", "u", "v", "single"),
    "FY": ("Y", "u", "vs", "pair"),
    "SX": ("Y", "un", "v", "single"),
    "FX": ("Y", "un", "vs", "pair"),
}
DETOURS = {"PY": "u", "PX": "un"}
NAMES = tuple(EVENTS) + tuple(n + h for n in DETOURS for h in "123")
N_EV = len(NAMES)
RELAY = {}
LONG = TOTAL
for _hop in "12":
    for _name in DETOURS:
        for _kind in "OQ":
            RELAY[_name + _hop, _kind] = LONG
            LONG += KEPT - CUT[_kind]
ORDER = (
    "R SZ O", "S FZ O", "R PZ O", "R PY1 O", "S PY2 O", "R Y O", "S SX O", "S PX1 O",
    "QY", "S Y Q", "S SY Q", "S PY1 Q", "S C0 O", "S Cs O", "S Cp O",
    "R FZ O", "S Cf O", "R PX1 O", "S PX2 O", "QZ", "S SZ Q", "S PZ Q",
    "R SY O", "S FY O", "R PY2 O", "S PY3 O", "R PY1 Q", "S PY2 Q",
    "R Y Q", "S SX Q", "S PX1 Q", "S C0 Q", "R SX O", "S FX O",
    "R FY O", "R PX2 O", "S PX3 O", "R PX1 Q", "S PX2 Q", "R PY2 Q", "S PY3 Q",
    "R SY Q", "S FY Q", "R SZ Q", "S FZ Q", "R PZ Q", "S Cs Q", "S Cp Q",
    "R C0 O", "R Cs O", "R PX2 Q", "S PX3 Q", "R FX O", "R PY3 O", "R PX3 O", "R Cp O",
    "R SX Q", "S FX Q", "R FZ Q", "S Cf Q", "R PY3 Q", "R Cf O",
    "R FY Q", "R C0 Q", "R PX3 Q", "R Cs Q", "R Cp Q", "R FX Q", "R Cf Q",
)


def gather_kernel(
    p_ref, h_ref, all_ref,
    ss, rs, ds, dr, loc, ins, inr, qs, qr, es, er, xs, xr,
):
    args = (p_ref, h_ref)
    g, d = lax.axis_index("grp"), lax.axis_index("dom")
    x, c = g // 2, g % 2
    z, y = d // 4, d % 4
    odd = x % 2
    u, v = y + odd * (z - y), z + odd * (y - z)
    host = u // 2
    near = {"u": u, "un": u + 1 - 2 * (u % 2)}
    far = v + 1 - 2 * (v % 2)
    ring = {"v": v, "vs": far, "vp": 3 - v, "vf": (3 - v) + 1 - 2 * ((3 - v) % 2)}

    def dom(uu, vv, swap=odd):
        return vv * 4 + uu + swap * 3 * (uu - vv)

    dq = dom(3 - u, v)
    sib_g = g + 1 - 2 * c
    sibling = (sib_g, d)
    aside, back = (g + GROUPS + 2 - 4 * c) % GROUPS, (g + GROUPS - 2 + 4 * c) % GROUPS
    ways = {
        "single": (g, dom(u, far)),
        "pair": (g, dom(u, 3 - v)),
        "cross": (g, dom(near["un"], v)),
        "1": (aside, d),
        "2": (g, dq),
        "3": (back, d),
    }
    is_own = (c + host + 1) % 2
    work_g = is_own * g + (1 - is_own) * sib_g
    work_d = is_own * d + (1 - is_own) * dq

    def worker(to):
        turned = (to // 2) % 2
        across = y + turned * (z - y)
        same = (across // 2 + to + 1) % 2
        there = d + (1 - turned) * (3 - 2 * y) + turned * 4 * (3 - 2 * z)
        return (
            same * to + (1 - same) * (to + 1 - 2 * (to % 2)),
            same * d + (1 - same) * there,
        )

    up_t, down_t = worker((g + 1) % GROUPS), worker((g + GROUPS - 1) % GROUPS)
    partner_idle = (2 * x + host, dq)

    barrier = pltpu.get_barrier_semaphore()
    for who in (
        *ways.values(), sibling, partner_idle,
        ((work_g + GROUPS - 1) % GROUPS, work_d), ((work_g + 1) % GROUPS, work_d),
    ):
        pl.semaphore_signal(barrier, inc=1, device_id=who, device_id_type=MESH)
    pl.semaphore_wait(barrier, 11 - 2 * is_own)

    def at(dom, row, lo, n):
        return all_ref.at[pl.ds((dom * 2 + row) * KEPT + lo, n)]

    def at1(dom, row, lo, n, a):
        return all_ref.at[pl.ds((dom * 2 + row) * KEPT + lo, n), a]

    def remote(src, dst, s, r, who):
        return pltpu.make_async_remote_copy(
            src_ref=src, dst_ref=dst, send_sem=s, recv_sem=r, device_id=who, device_id_type=MESH
        )

    def init_copies(row, to):
        out = []
        for k, (s0, s1, b) in enumerate(PARTS):
            for a in range(2):
                src = args[a].at[row, pl.ds(s0, s1 - s0)]
                dst = at1(d, row, b, s1 - s0, a)
                if to == "own":
                    out.append(pltpu.make_async_copy(src, dst, loc.at[row, k, a]))
                elif to == "sibling":
                    out.append(remote(src, dst, ins.at[row, k, a], inr.at[row, k, a], sibling))
                else:
                    out.append(remote(src, dst, qs.at[row, k, a], qr.at[k, a], (2 * x + row, dq)))
        return out

    def extra_copies(to):
        out = []
        for row in range(2):
            for a in range(2):
                src = args[a].at[row, pl.ds(1, 2)]
                dst = all_ref.at[pl.ds(EXTRA + 2 * row, 2), a]
                if to == "own":
                    out.append(pltpu.make_async_copy(src, dst, es.at[row, a]))
                else:
                    out.append(remote(src, dst, es.at[row, a], er.at[row, a], (sib_g, dq)))
        return out

    def side_copies():
        out = []
        for k, who in enumerate((up_t, down_t)):
            for row in range(2):
                for a in range(2):
                    src = args[a].at[row, pl.ds(0, 3)]
                    dst = all_ref.at[pl.ds(EXTRA + 4 + 6 * k + 3 * row, 3), a]
                    out.append(remote(src, dst, xs.at[k, row, a], xr.at[k, row, a], who))
        return out

    own = c == host
    for core in range(2):

        @pl.when(jnp.logical_and(own, c == core))
        def _():
            mine = init_copies(core, "own")
            theirs = init_copies(1 - core, "sibling")
            for m, t in zip(mine, theirs):
                m.start()
                t.start()
            for copy in init_copies(core, "sibling") + init_copies(1 - core, "own"):
                copy.start()
            for copy in mine:
                copy.wait()

        @pl.when(jnp.logical_and(jnp.logical_not(own), c == core))
        def _():
            for m, t in zip(init_copies(0, "partner"), init_copies(1, "partner")):
                m.start()
                t.start()
            for copy in init_copies(core, "sibling"):
                copy.wait_recv()

    def turn(uu, kind):
        return uu if kind == "O" else 3 - uu

    seen_by = {
        "single": {"v": "vs"},
        "pair": {"v": "vp", "vs": "vf"},
        "cross": {"v": "v", "vs": "vs", "vp": "vp", "vf": "vf"},
    }

    def event(name, kind, side):
        k = NAMES.index(name) + (N_EV if kind == "Q" else 0)
        cut = CUT[kind]
        n = KEPT - cut
        if name in EVENTS:
            part, col, place, way = EVENTS[name]
            if side == "R":
                place = seen_by[way][place]
                if way == "cross":
                    col = "un"
            lo, n = (0, cut) if part == "Z" else (cut, n)
            owner = dom(turn(near[col], kind), ring[place])
            src = dst = at(owner, c, lo, n)
            what = (owner, lo, n, k)
        else:
            way, base = name[2], name[:2]
            col = DETOURS[base]
            what = None
            relay = {h: all_ref.at[pl.ds(RELAY[base + h, kind], n)] for h in "12"}
            if way == "3" and side == "R":
                owner = dom(turn(near[col], kind), 3 - v)
                src = dst = at(owner, c, cut, n)
                what = (owner, cut, n, k)
            elif way == "3":
                owner = dom(turn({"u": v, "un": far}[col], kind), 3 - u, 1 - odd)
                src, dst = relay["2"], at(owner, c, cut, n)
            elif way == "2":
                src, dst = relay["1"], relay["2"]
            else:
                src, dst = at(dom(turn(near[col], kind), v), c, cut, n), relay["1"]
        return remote(src, dst, ss.at[k], rs.at[k], ways[way]), what

    passed = []

    def to_sibling(dom, lo, n, k):
        ref = at(dom, c, lo, n)
        remote(ref, ref, ds.at[k], dr.at[k], sibling).start()
        passed.append((dom, lo, n, k))

    sent = []

    def send(name, kind):
        copy, _ = event(name, kind, "S")
        copy.start()
        sent.append(copy)

    def receive(name, kind):
        copy, what = event(name, kind, "R")
        copy.wait_recv()
        if what is not None:
            to_sibling(*what)

    def receive_partner(parts, lo, n, k):
        for part in parts:
            s0, s1, b = PARTS[part]
            for a in range(2):
                ref = at1(dq, c, b, s1 - s0, a)
                remote(ref, ref, qs.at[0, part, a], qr.at[part, a], sibling).wait_recv()
        to_sibling(dq, lo, n, k)

    for name in ("Y", "SZ", "PZ", "SY", "PY1"):
        send(name, "O")

    sides = side_copies()
    for copy in sides:
        copy.start()

    @pl.when(own)
    def _():
        for copy in extra_copies("own"):
            copy.start()

    @pl.when(jnp.logical_not(own))
    def _():
        for copy in extra_copies("partner"):
            copy.start()

    for step in ORDER:
        if step == "QY":
            receive_partner((0,), CUT["Q"], KEPT - CUT["Q"], 2 * N_EV)
        elif step == "QZ":
            receive_partner((1, 2), 0, CUT["Q"], 2 * N_EV + 1)
        else:
            what, name, kind = step.split()
            (send if what == "S" else receive)(name, kind)

    for core in range(2):

        @pl.when(jnp.logical_and(own, c == core))
        def _():
            for copy in init_copies(1 - core, "own") + extra_copies("own"):
                copy.wait()
            for copy in init_copies(0, "sibling") + init_copies(1, "sibling"):
                copy.wait_send()

        @pl.when(jnp.logical_and(jnp.logical_not(own), c == core))
        def _():
            for copy in init_copies(1 - core, "sibling"):
                copy.wait_recv()
            for copy in init_copies(0, "partner") + init_copies(1, "partner"):
                copy.wait_send()
            for copy in extra_copies("partner"):
                copy.wait()

    for copy in sides:
        copy.wait()
    for copy in sent:
        copy.wait_send()
    for dom, lo, n, k in passed:
        mine, theirs = at(dom, c, lo, n), at(dom, 1 - c, lo, n)
        remote(mine, mine, ds.at[k], dr.at[k], sibling).wait_send()
        remote(theirs, theirs, ds.at[k], dr.at[k], sibling).wait_recv()


def gather(density, hamiltonian):
    dma = pltpu.SemaphoreType.DMA
    return pl.pallas_call(
        gather_kernel,
        name="gather",
        out_shape=jax.ShapeDtypeStruct((LONG, 2, BLK, BLK), jnp.bfloat16),
        in_specs=[pl.BlockSpec(memory_space=pl.ANY)] * 2,
        out_specs=pl.BlockSpec(memory_space=pl.ANY),
        scratch_shapes=[
            dma((2 * N_EV,)), dma((2 * N_EV,)), dma((2 * N_EV + 2,)), dma((2 * N_EV + 2,)),
            dma((2, 3, 2)), dma((2, 3, 2)), dma((2, 3, 2)), dma((2, 3, 2)), dma((3, 2)),
            dma((2, 2)), dma((2, 2)), dma((2, 2, 2)), dma((2, 2, 2)),
        ],
        compiler_params=pltpu.CompilerParams(collective_id=0, has_side_effects=True),
    )(density, hamiltonian)


def row_kernel(
    steps, chunk_s, slots, places, mine, all_ref, x_ref, g_ref, send_ref,
    left, right, low, high, mid, sem_a, sem_b,
):
    def fetch_left(lo, n, at):
        return pltpu.make_async_copy(
            all_ref.at[pl.ds(at, n)], left.at[pl.ds(lo, n)], sem_a.at[lo // KEPT]
        )

    def fetch(e):
        return pltpu.make_async_copy(all_ref.at[places[e]], right.at[e], sem_b.at[e])

    def fetch_step(q, what):
        for k in range(STEP * CHUNK):
            what(fetch(q * (STEP * CHUNK) + k))

    a_copies = (fetch_left(0, KEPT, mine[0]), fetch_left(KEPT, 2, mine[1]))
    for copy in a_copies:
        copy.start()

    @pl.loop(0, steps[0])
    def _(q):
        fetch_step(q, lambda copy: copy.start())

    left[NNZ] = jnp.zeros((2, BLK, BLK), jnp.bfloat16)
    mid[NNZ] = jnp.zeros((2, BLK, BLK), jnp.bfloat16)
    for s in range(NNZ):
        low[s] = jnp.zeros((BLK, 2 * BLK), jnp.float32)
        high[s] = jnp.zeros((BLK, 2 * BLK), jnp.float32)
    for copy in a_copies:
        copy.wait()

    def step(q, a_ref, total):
        sums = []
        for k in range(STEP):
            first = (q * STEP + k) * CHUNK
            e = [first + p for p in range(CHUNK)]
            t = [slots[p] for p in e]
            a = jnp.concatenate([a_ref[p, 0] for p in t], axis=1)
            b = jnp.concatenate([a_ref[p, 1] for p in t], axis=1)
            den = jnp.concatenate([right[p, 0] for p in e], axis=0)
            ham = jnp.concatenate([right[p, 1] for p in e], axis=0)
            both = jnp.dot(a, jnp.concatenate([den, ham], axis=1), preferred_element_type=jnp.float32)
            more = jnp.dot(b, den, preferred_element_type=jnp.float32)
            sums.append((both, more))
        for k in range(STEP):
            s = chunk_s[q * STEP + k]
            both, more = sums[k]
            total[s, :, :BLK] += both[:, :BLK]
            total[s, :, BLK:] += both[:, BLK:] + more

    @pl.loop(0, steps[0])
    def _(q):
        fetch_step(q, lambda copy: copy.wait())
        step(q, left, low)

    for s in range(NNZ):
        at = 0 if s == 0 else KEPT - 1 + s if s < 3 else s - 2
        mid[at, 0] = low[s, :, :BLK].astype(jnp.bfloat16)
        mid[at, 1] = low[s, :, BLK:].astype(jnp.bfloat16)

    @pl.loop(0, steps[0])
    def _(q):
        step(q, mid, high)

    for s in range(NNZ):
        purified = 3.0 * low[s, :, :BLK] - 2.0 * high[s, :, :BLK]
        gradient = 3.0 * low[s, :, BLK:] - 2.0 * high[s, :, BLK:]
        x_ref[s] = purified
        g_ref[s] = gradient
        send_ref[0, s] = purified.astype(jnp.bfloat16)
        send_ref[1, s] = gradient.astype(jnp.bfloat16)


def one_row(name, steps, chunk_s, slots, places, mine, everything):
    f32, bf16 = jnp.float32, jnp.bfloat16
    vmem = pl.BlockSpec(memory_space=pltpu.VMEM)
    smem = pl.BlockSpec(memory_space=pltpu.SMEM)
    return pl.pallas_call(
        row_kernel,
        name=name,
        out_shape=(
            jax.ShapeDtypeStruct((NNZ, BLK, BLK), f32),
            jax.ShapeDtypeStruct((NNZ, BLK, BLK), f32),
            jax.ShapeDtypeStruct((2, NNZ, BLK, BLK), bf16),
        ),
        in_specs=[smem] * 5 + [pl.BlockSpec(memory_space=pl.ANY)],
        out_specs=(vmem, vmem, vmem),
        scratch_shapes=[
            pltpu.VMEM((NNZ + 1, 2, BLK, BLK), bf16),
            pltpu.VMEM((ENTRIES, 2, BLK, BLK), bf16),
            pltpu.VMEM((NNZ + 1, BLK, 2 * BLK), f32),
            pltpu.VMEM((NNZ + 1, BLK, 2 * BLK), f32),
            pltpu.VMEM((NNZ + 1, 2, BLK, BLK), bf16),
            pltpu.SemaphoreType.DMA((2,)),
            pltpu.SemaphoreType.DMA((ENTRIES,)),
        ],
        compiler_params=pltpu.CompilerParams(vmem_limit_bytes=40 << 20),
        cost_estimate=pl.CostEstimate(
            flops=2 * 2 * 3 * 104 * BLK**3, bytes_accessed=14 << 20, transcendentals=0
        ),
    )(steps, chunk_s, slots, places, mine, everything)


def tables(pattern, work_g, work_d):
    first = work_g * SPAN + work_d * 2
    cols = lax.dynamic_slice_in_dim(pattern, first, 2, 0)
    far = jnp.take(pattern, cols, axis=0)
    slot = jnp.arange(NNZ, dtype=jnp.int32)
    found = jnp.max(
        jnp.where(far[:, :, None, :] == cols[:, None, :, None], slot + 1, 0), axis=3
    ) - 1
    group, inner = cols // SPAN, cols % SPAN
    row = cols % 2
    inside = (group == work_g)[:, :, None]
    before = (group == (work_g + GROUPS - 1) % GROUPS)[:, :, None]
    short = jnp.clip(found, 0, 2)
    place = jnp.where(
        inside,
        jnp.where(
            (found == 1) | (found == 2),
            EXTRA + 2 * row[:, :, None] + jnp.clip(found - 1, 0, 1),
            inner[:, :, None] * KEPT + jnp.where(found < 3, 0, found - 2),
        ),
        EXTRA + 4 + 3 * row[:, :, None] + short + jnp.where(before, 0, 6),
    )
    hit = found >= 0
    held = hit.astype(jnp.int32)
    count = jnp.sum(held, axis=1)
    rank = jnp.sum(jnp.where(slot[None, :, None, None] > slot[None, None, :, None], held[:, None], 0), axis=2)
    chunks = (count + CHUNK - 1) // CHUNK
    start = jnp.sum(jnp.where(slot[None, None, :] < slot[None, :, None], chunks[:, None, :], 0), axis=2)
    spot = jnp.where(hit, start[:, None, :] * CHUNK + rank, -1).reshape(2, 1, NNZ * NNZ)
    chosen = spot == jnp.arange(ENTRIES, dtype=jnp.int32)[None, :, None]
    left_at = jnp.where(slot == 0, 0, jnp.where(slot < 3, KEPT - 1 + slot, slot - 2))
    both = jnp.broadcast_to(left_at[None, :, None] - NNZ, found.shape) + place * 32
    both = jnp.sum(jnp.where(chosen, both.reshape(2, 1, NNZ * NNZ) + NNZ, 0), axis=2)
    slots = jnp.where(jnp.any(chosen, axis=2), both % 32, NNZ)
    places = both // 32
    c = jnp.arange(ENTRIES // CHUNK, dtype=jnp.int32)[None, :, None]
    chunk_s = jnp.sum((c >= (start + chunks)[:, None, :]).astype(jnp.int32), axis=2)
    steps = (jnp.sum(chunks, axis=1, keepdims=True) + STEP - 1) // STEP
    return steps, chunk_s, slots, places


def on_device(pattern, density, hamiltonian):
    g, d = lax.axis_index("grp"), lax.axis_index("dom")
    odd = g // 2 % 2
    u = jnp.where(odd == 1, d // 4, d % 4)
    own = g % 2 == u // 2
    work_g = jnp.where(own, g, g + 1 - 2 * (g % 2))
    work_d = jnp.where(own, d, d + jnp.where(odd == 1, 4, 1) * (3 - 2 * u))
    lists = tables(pattern, work_g, work_d)
    everything = gather(density, hamiltonian)
    pairs = []
    for gg in range(8):
        for dd in range(16):
            uu, unit = (dd // 4, 4) if gg // 2 % 2 else (dd % 4, 1)
            if gg % 2 != uu // 2:
                pairs.append((gg * 16 + dd, (gg ^ 1) * 16 + dd + unit * (3 - 2 * uu)))
    mine, back = [], []
    for w in range(2):
        where = jnp.stack([(work_d * 2 + w) * KEPT, jnp.int32(EXTRA + 2 * w)])
        px, gx, out = one_row(f"row{w}", *(v[w] for v in lists), where, everything)
        mine.append((px, gx))
        back.append(lax.ppermute(out, ("grp", "dom"), pairs))
    res = []
    for k in range(2):
        res.append(jnp.stack([
            jnp.where(own, mine[w][k], back[w][k].astype(jnp.float32)) for w in range(2)
        ]))
    return tuple(res)


def solution(mesh):
    split = P(("grp", "dom"), None, None, None)
    return jax.shard_map(
        on_device,
        mesh=mesh,
        in_specs=(P(), split, split),
        out_specs=(split, split),
        check_vma=False,
    )
```

```python
import functools

import jax
import jax.numpy as jnp
from jax import lax
from jax.experimental import pallas as pl
from jax.experimental.pallas import tpu as pltpu
from jax.sharding import PartitionSpec as P

MESH = pl.DeviceIdType.MESH
BLK = 128
NNZ = 16
KEPT = 14
SPAN = 32
GROUPS = 8
EXTRA = SPAN * KEPT
TOTAL = EXTRA + 4 + 6 + 6
CHUNK = 2
STEP = 8
ENTRIES = NNZ * NNZ
CUT = {"O": 6, "Q": 4}
PARTS = ((CUT["Q"] + 2, NNZ, CUT["Q"]), (0, 1, 0), (3, CUT["Q"] + 2, 1))

EVENTS = {
    "SZ": ("Z", "u", "v", "single"),
    "PZ": ("Z", "u", "v", "pair"),
    "FZ": ("Z", "u", "vs", "pair"),
    "C0": ("Z", "u", "v", "cross"),
    "Cs": ("Z", "u", "vs", "cross"),
    "Cp": ("Z", "u", "vp", "cross"),
    "Cf": ("Z", "u", "vf", "cross"),
    "Y": ("Y", "u", "v", "cross"),
    "SY": ("Y", "u", "v", "single"),
    "FY": ("Y", "u", "vs", "pair"),
    "SX": ("Y", "un", "v", "single"),
    "FX": ("Y", "un", "vs", "pair"),
}
DETOURS = {"PY": "u", "PX": "un"}
NAMES = tuple(EVENTS) + tuple(n + h for n in DETOURS for h in "123")
N_EV = len(NAMES)
RELAY = {}
LONG = TOTAL
for _hop in "12":
    for _name in DETOURS:
        for _kind in "OQ":
            RELAY[_name + _hop, _kind] = LONG
            LONG += KEPT - CUT[_kind]
ORDER = (
    "S SY O", "S Y O", "S PY1 O", "S PZ O", "S C0 O", "R SY O", "S SZ O", "S FY O",
    "QY", "QZ", "R PY1 O", "S SZ Q", "S PY1 Q", "S Y Q", "S PY2 O", "R SZ O",
    "S PZ Q", "R Y O", "S SY Q", "S FZ O", "R PY1 Q", "R SZ Q", "S C0 Q", "S FZ Q",
    "S PY2 Q", "S PX1 O", "R Y Q", "S SX O", "S Cs Q", "R PZ O", "S Cs O", "R SY Q",
    "S FY Q", "S PX1 Q", "R C0 Q", "R PX1 O", "S PX2 O", "R PZ Q", "S Cp O", "R SX O",
    "R PY2 O", "R FY O", "R PY2 Q", "S Cp Q", "S PY3 O", "S SX Q", "S PY3 Q", "R Cs Q",
    "R FZ O", "R PX1 Q", "S PX2 Q", "S FX O", "R PX2 O", "R SX Q", "S Cf O", "S FX Q",
    "R FZ Q", "R Cp O", "R Cs O", "S PX3 O", "R PY3 Q", "SIDES", "S Cf Q", "R PX2 Q",
    "S PX3 Q", "R FX Q", "R PX3 Q", "R C0 O", "R PY3 O", "R Cf Q", "R FX O", "R Cf O",
    "R PX3 O", "R FY Q", "R Cp Q",
)


def gather_kernel(
    p_ref, h_ref, all_ref,
    ss, rs, ds, dr, loc, ins, inr, qs, qr, es, er, xs, xr,
):
    args = (p_ref, h_ref)
    g, d = lax.axis_index("grp"), lax.axis_index("dom")
    x, c = g // 2, g % 2
    z, y = d // 4, d % 4
    odd = x % 2
    u, v = y + odd * (z - y), z + odd * (y - z)
    host = u // 2
    near = {"u": u, "un": u + 1 - 2 * (u % 2)}
    far = v + 1 - 2 * (v % 2)
    ring = {"v": v, "vs": far, "vp": 3 - v, "vf": (3 - v) + 1 - 2 * ((3 - v) % 2)}

    def dom(uu, vv, swap=odd):
        return vv * 4 + uu + swap * 3 * (uu - vv)

    dq = dom(3 - u, v)
    sib_g = g + 1 - 2 * c
    sibling = (sib_g, d)
    aside, back = (g + GROUPS + 2 - 4 * c) % GROUPS, (g + GROUPS - 2 + 4 * c) % GROUPS
    ways = {
        "single": (g, dom(u, far)),
        "pair": (g, dom(u, 3 - v)),
        "cross": (g, dom(near["un"], v)),
        "1": (aside, d),
        "2": (g, dq),
        "3": (back, d),
    }
    is_own = (c + host + 1) % 2
    work_g = is_own * g + (1 - is_own) * sib_g
    work_d = is_own * d + (1 - is_own) * dq

    def worker(to):
        turned = (to // 2) % 2
        across = y + turned * (z - y)
        same = (across // 2 + to + 1) % 2
        there = d + (1 - turned) * (3 - 2 * y) + turned * 4 * (3 - 2 * z)
        return (
            same * to + (1 - same) * (to + 1 - 2 * (to % 2)),
            same * d + (1 - same) * there,
        )

    up_t, down_t = worker((g + 1) % GROUPS), worker((g + GROUPS - 1) % GROUPS)
    partner_idle = (2 * x + host, dq)

    barrier = pltpu.get_barrier_semaphore()
    for who in (
        *ways.values(), sibling, partner_idle,
        ((work_g + GROUPS - 1) % GROUPS, work_d), ((work_g + 1) % GROUPS, work_d),
    ):
        pl.semaphore_signal(barrier, inc=1, device_id=who, device_id_type=MESH)
    pl.semaphore_wait(barrier, 11 - 2 * is_own)

    def at(dom, row, lo, n):
        return all_ref.at[pl.ds((dom * 2 + row) * KEPT + lo, n)]

    def at1(dom, row, lo, n, a):
        return all_ref.at[pl.ds((dom * 2 + row) * KEPT + lo, n), a]

    def remote(src, dst, s, r, who):
        return pltpu.make_async_remote_copy(
            src_ref=src, dst_ref=dst, send_sem=s, recv_sem=r, device_id=who, device_id_type=MESH
        )

    def init_copies(row, to):
        out = []
        for k, (s0, s1, b) in enumerate(PARTS):
            for a in range(2):
                src = args[a].at[row, pl.ds(s0, s1 - s0)]
                dst = at1(d, row, b, s1 - s0, a)
                if to == "own":
                    out.append(pltpu.make_async_copy(src, dst, loc.at[row, k, a]))
                elif to == "sibling":
                    out.append(remote(src, dst, ins.at[row, k, a], inr.at[row, k, a], sibling))
                else:
                    out.append(remote(src, dst, qs.at[row, k, a], qr.at[k, a], (2 * x + row, dq)))
        return out

    def extra_copies(to):
        out = []
        for row in range(2):
            for a in range(2):
                src = args[a].at[row, pl.ds(1, 2)]
                dst = all_ref.at[pl.ds(EXTRA + 2 * row, 2), a]
                if to == "own":
                    out.append(pltpu.make_async_copy(src, dst, es.at[row, a]))
                else:
                    out.append(remote(src, dst, es.at[row, a], er.at[row, a], (sib_g, dq)))
        return out

    def side_copies():
        out = []
        for k, who in enumerate((up_t, down_t)):
            for row in range(2):
                for a in range(2):
                    src = args[a].at[row, pl.ds(0, 3)]
                    dst = all_ref.at[pl.ds(EXTRA + 4 + 6 * k + 3 * row, 3), a]
                    out.append(remote(src, dst, xs.at[k, row, a], xr.at[k, row, a], who))
        return out

    own = c == host
    for core in range(2):

        @pl.when(jnp.logical_and(own, c == core))
        def _():
            mine = init_copies(core, "own")
            theirs = init_copies(1 - core, "sibling")
            for m, t in zip(mine, theirs):
                m.start()
                t.start()
            for copy in init_copies(core, "sibling") + init_copies(1 - core, "own"):
                copy.start()
            for copy in mine:
                copy.wait()

        @pl.when(jnp.logical_and(jnp.logical_not(own), c == core))
        def _():
            for m, t in zip(init_copies(0, "partner"), init_copies(1, "partner")):
                m.start()
                t.start()
            for copy in init_copies(core, "sibling"):
                copy.wait_recv()

    def turn(uu, kind):
        return uu if kind == "O" else 3 - uu

    seen_by = {
        "single": {"v": "vs"},
        "pair": {"v": "vp", "vs": "vf"},
        "cross": {"v": "v", "vs": "vs", "vp": "vp", "vf": "vf"},
    }

    def event(name, kind, side):
        k = NAMES.index(name) + (N_EV if kind == "Q" else 0)
        cut = CUT[kind]
        n = KEPT - cut
        if name in EVENTS:
            part, col, place, way = EVENTS[name]
            if side == "R":
                place = seen_by[way][place]
                if way == "cross":
                    col = "un"
            lo, n = (0, cut) if part == "Z" else (cut, n)
            owner = dom(turn(near[col], kind), ring[place])
            src = dst = at(owner, c, lo, n)
            what = (owner, lo, n, k)
        else:
            way, base = name[2], name[:2]
            col = DETOURS[base]
            what = None
            relay = {h: all_ref.at[pl.ds(RELAY[base + h, kind], n)] for h in "12"}
            if way == "3" and side == "R":
                owner = dom(turn(near[col], kind), 3 - v)
                src = dst = at(owner, c, cut, n)
                what = (owner, cut, n, k)
            elif way == "3":
                owner = dom(turn({"u": v, "un": far}[col], kind), 3 - u, 1 - odd)
                src, dst = relay["2"], at(owner, c, cut, n)
            elif way == "2":
                src, dst = relay["1"], relay["2"]
            else:
                src, dst = at(dom(turn(near[col], kind), v), c, cut, n), relay["1"]
        return remote(src, dst, ss.at[k], rs.at[k], ways[way]), what

    passed = []

    def to_sibling(dom, lo, n, k):
        ref = at(dom, c, lo, n)
        remote(ref, ref, ds.at[k], dr.at[k], sibling).start()
        passed.append((dom, lo, n, k))

    sent = []

    def send(name, kind):
        copy, _ = event(name, kind, "S")
        copy.start()
        sent.append(copy)

    def receive(name, kind):
        copy, what = event(name, kind, "R")
        copy.wait_recv()
        if what is not None:
            to_sibling(*what)

    def receive_partner(parts, lo, n, k):
        for part in parts:
            s0, s1, b = PARTS[part]
            for a in range(2):
                ref = at1(dq, c, b, s1 - s0, a)
                remote(ref, ref, qs.at[0, part, a], qr.at[part, a], sibling).wait_recv()
        to_sibling(dq, lo, n, k)

    sides = side_copies()

    def start_sides():
        for copy in sides:
            copy.start()

        @pl.when(own)
        def _():
            for copy in extra_copies("own"):
                copy.start()

        @pl.when(jnp.logical_not(own))
        def _():
            for copy in extra_copies("partner"):
                copy.start()

    for step in ORDER:
        if step == "SIDES":
            start_sides()
        elif step == "QY":
            receive_partner((0,), CUT["Q"], KEPT - CUT["Q"], 2 * N_EV)
        elif step == "QZ":
            receive_partner((1, 2), 0, CUT["Q"], 2 * N_EV + 1)
        else:
            what, name, kind = step.split()
            (send if what == "S" else receive)(name, kind)

    for core in range(2):

        @pl.when(jnp.logical_and(own, c == core))
        def _():
            for copy in init_copies(1 - core, "own") + extra_copies("own"):
                copy.wait()
            for copy in init_copies(0, "sibling") + init_copies(1, "sibling"):
                copy.wait_send()

        @pl.when(jnp.logical_and(jnp.logical_not(own), c == core))
        def _():
            for copy in init_copies(1 - core, "sibling"):
                copy.wait_recv()
            for copy in init_copies(0, "partner") + init_copies(1, "partner"):
                copy.wait_send()
            for copy in extra_copies("partner"):
                copy.wait()

    for copy in sides:
        copy.wait()
    for copy in sent:
        copy.wait_send()
    for dom, lo, n, k in passed:
        mine, theirs = at(dom, c, lo, n), at(dom, 1 - c, lo, n)
        remote(mine, mine, ds.at[k], dr.at[k], sibling).wait_send()
        remote(theirs, theirs, ds.at[k], dr.at[k], sibling).wait_recv()


def gather(density, hamiltonian):
    dma = pltpu.SemaphoreType.DMA
    return pl.pallas_call(
        gather_kernel,
        name="gather",
        out_shape=jax.ShapeDtypeStruct((LONG, 2, BLK, BLK), jnp.bfloat16),
        in_specs=[pl.BlockSpec(memory_space=pl.ANY)] * 2,
        out_specs=pl.BlockSpec(memory_space=pl.ANY),
        scratch_shapes=[
            dma((2 * N_EV,)), dma((2 * N_EV,)), dma((2 * N_EV + 2,)), dma((2 * N_EV + 2,)),
            dma((2, 3, 2)), dma((2, 3, 2)), dma((2, 3, 2)), dma((2, 3, 2)), dma((3, 2)),
            dma((2, 2)), dma((2, 2)), dma((2, 2, 2)), dma((2, 2, 2)),
        ],
        compiler_params=pltpu.CompilerParams(collective_id=0, has_side_effects=True),
    )(density, hamiltonian)


def row_kernel(w, *refs):
    steps, chunk_s, slots, places, mine, all_ref = refs[:6]
    x_ref, g_ref, send_ref = refs[6 + 2 * w : 9 + 2 * w]
    left, right, low, high, mid, full, short, sem_a, sem_b, sem_o = refs[9 + 2 * w :]

    def fetch_left(lo, n, at):
        return pltpu.make_async_copy(
            all_ref.at[pl.ds(at, n)], left.at[pl.ds(lo, n)], sem_a.at[lo // KEPT]
        )

    def fetch(e):
        return pltpu.make_async_copy(all_ref.at[places[e]], right.at[e], sem_b.at[e])

    def fetch_step(q, what):
        for k in range(STEP * CHUNK):
            what(fetch(q * (STEP * CHUNK) + k))

    a_copies = (fetch_left(0, KEPT, mine[0]), fetch_left(KEPT, 2, mine[1]))
    for copy in a_copies:
        copy.start()

    @pl.loop(0, steps[0])
    def _(q):
        fetch_step(q, lambda copy: copy.start())

    left[NNZ] = jnp.zeros((2, BLK, BLK), jnp.bfloat16)
    mid[NNZ] = jnp.zeros((2, BLK, BLK), jnp.bfloat16)
    for s in range(NNZ):
        low[s] = jnp.zeros((BLK, 2 * BLK), jnp.float32)
        high[s] = jnp.zeros((BLK, 2 * BLK), jnp.float32)
    for copy in a_copies:
        copy.wait()

    def step(q, a_ref, total):
        sums = []
        for k in range(STEP):
            first = (q * STEP + k) * CHUNK
            e = [first + p for p in range(CHUNK)]
            t = [slots[p] for p in e]
            a = jnp.concatenate([a_ref[p, 0] for p in t], axis=1)
            b = jnp.concatenate([a_ref[p, 1] for p in t], axis=1)
            den = jnp.concatenate([right[p, 0] for p in e], axis=0)
            ham = jnp.concatenate([right[p, 1] for p in e], axis=0)
            both = jnp.dot(a, jnp.concatenate([den, ham], axis=1), preferred_element_type=jnp.float32)
            more = jnp.dot(b, den, preferred_element_type=jnp.float32)
            sums.append((both, more))
        for k in range(STEP):
            s = chunk_s[q * STEP + k]
            both, more = sums[k]
            total[s, :, :BLK] += both[:, :BLK]
            total[s, :, BLK:] += both[:, BLK:] + more

    @pl.loop(0, steps[0])
    def _(q):
        fetch_step(q, lambda copy: copy.wait())
        step(q, left, low)

    for s in range(NNZ):
        at = 0 if s == 0 else KEPT - 1 + s if s < 3 else s - 2
        mid[at, 0] = low[s, :, :BLK].astype(jnp.bfloat16)
        mid[at, 1] = low[s, :, BLK:].astype(jnp.bfloat16)

    @pl.loop(0, steps[0])
    def _(q):
        step(q, mid, high)

    def finished(keep):
        out = []
        for s in range(NNZ):
            for k, ref in enumerate((x_ref, g_ref)):
                part = pl.ds(k * BLK, BLK)
                value = 3.0 * low[s, :, part] - 2.0 * high[s, :, part]
                if keep:
                    full[k, s] = value
                else:
                    short[k, s] = value.astype(jnp.bfloat16)
                if s % 4 == 3:
                    some = pl.ds(s - 3, 4)
                    sem = sem_o.at[k, s // 4]
                    out.append(
                        pltpu.make_async_copy(full.at[k, some], ref.at[w, some], sem)
                        if keep
                        else pltpu.make_async_copy(short.at[k, some], send_ref.at[k, some], sem)
                    )
                    out[-1].start()
        for copy in out:
            copy.wait()

    pl.when(mine[2] == 1)(lambda: finished(True))
    pl.when(mine[2] == 0)(lambda: finished(False))


WHOLE = jax.ShapeDtypeStruct((2, NNZ, BLK, BLK), jnp.float32)
HALF = jax.ShapeDtypeStruct((2, NNZ, BLK, BLK), jnp.bfloat16)


def one_row(w, steps, chunk_s, slots, places, mine, everything, *before):
    f32, bf16 = jnp.float32, jnp.bfloat16
    anywhere = pl.BlockSpec(memory_space=pl.ANY)
    smem = pl.BlockSpec(memory_space=pltpu.SMEM)
    return pl.pallas_call(
        functools.partial(row_kernel, w),
        name=f"row{w}",
        out_shape=(WHOLE, WHOLE, HALF),
        in_specs=[smem] * 5 + [anywhere] * (1 + len(before)),
        out_specs=(anywhere,) * 3,
        input_output_aliases={6 + k: k for k in range(len(before))},
        scratch_shapes=[
            pltpu.VMEM((NNZ + 1, 2, BLK, BLK), bf16),
            pltpu.VMEM((ENTRIES, 2, BLK, BLK), bf16),
            pltpu.VMEM((NNZ + 1, BLK, 2 * BLK), f32),
            pltpu.VMEM((NNZ + 1, BLK, 2 * BLK), f32),
            pltpu.VMEM((NNZ + 1, 2, BLK, BLK), bf16),
            pltpu.VMEM((2, NNZ, BLK, BLK), f32),
            pltpu.VMEM((2, NNZ, BLK, BLK), bf16),
            pltpu.SemaphoreType.DMA((2,)),
            pltpu.SemaphoreType.DMA((ENTRIES,)),
            pltpu.SemaphoreType.DMA((2, 4)),
        ],
        compiler_params=pltpu.CompilerParams(vmem_limit_bytes=40 << 20),
        cost_estimate=pl.CostEstimate(
            flops=2 * 2 * 3 * 104 * BLK**3, bytes_accessed=14 << 20, transcendentals=0
        ),
    )(steps, chunk_s, slots, places, mine, everything, *before)


def finish_kernel(w, mine, back, x_in, g_in, x_ref, g_ref, short, full, sem_i, sem_o):
    @pl.when(mine[2] == 0)
    def _():
        def load(k, q):
            some = pl.ds(4 * q, 4)
            return pltpu.make_async_copy(back.at[k, some], short.at[k, some], sem_i.at[k, q])

        def store(k, q):
            some = pl.ds(4 * q, 4)
            ref = (x_ref, g_ref)[k]
            return pltpu.make_async_copy(full.at[k, some], ref.at[w, some], sem_o.at[k, q])

        parts = [(k, q) for k in range(2) for q in range(4)]
        for part in parts:
            load(*part).start()
        for k, q in parts:
            load(k, q).wait()
            full[k, 4 * q : 4 * q + 4] = short[k, 4 * q : 4 * q + 4].astype(jnp.float32)
            store(k, q).start()
        for part in parts:
            store(*part).wait()


def finish(w, mine, back, x, g):
    anywhere = pl.BlockSpec(memory_space=pl.ANY)
    return pl.pallas_call(
        functools.partial(finish_kernel, w),
        name=f"finish{w}",
        out_shape=(WHOLE, WHOLE),
        in_specs=[pl.BlockSpec(memory_space=pltpu.SMEM)] + [anywhere] * 3,
        out_specs=(anywhere,) * 2,
        input_output_aliases={2: 0, 3: 1},
        scratch_shapes=[
            pltpu.VMEM((2, NNZ, BLK, BLK), jnp.bfloat16),
            pltpu.VMEM((2, NNZ, BLK, BLK), jnp.float32),
            pltpu.SemaphoreType.DMA((2, 4)),
            pltpu.SemaphoreType.DMA((2, 4)),
        ],
        compiler_params=pltpu.CompilerParams(vmem_limit_bytes=16 << 20),
        cost_estimate=pl.CostEstimate(flops=1 << 20, bytes_accessed=3 << 20, transcendentals=0),
    )(mine, back, x, g)


def tables(pattern, work_g, work_d):
    first = work_g * SPAN + work_d * 2
    cols = lax.dynamic_slice_in_dim(pattern, first, 2, 0)
    far = jnp.take(pattern, cols, axis=0)
    slot = jnp.arange(NNZ, dtype=jnp.int32)
    found = jnp.max(
        jnp.where(far[:, :, None, :] == cols[:, None, :, None], slot + 1, 0), axis=3
    ) - 1
    group, inner = cols // SPAN, cols % SPAN
    row = cols % 2
    inside = (group == work_g)[:, :, None]
    before = (group == (work_g + GROUPS - 1) % GROUPS)[:, :, None]
    short = jnp.clip(found, 0, 2)
    place = jnp.where(
        inside,
        jnp.where(
            (found == 1) | (found == 2),
            EXTRA + 2 * row[:, :, None] + jnp.clip(found - 1, 0, 1),
            inner[:, :, None] * KEPT + jnp.where(found < 3, 0, found - 2),
        ),
        EXTRA + 4 + 3 * row[:, :, None] + short + jnp.where(before, 0, 6),
    )
    hit = found >= 0
    held = hit.astype(jnp.int32)
    count = jnp.sum(held, axis=1)
    rank = jnp.sum(jnp.where(slot[None, :, None, None] > slot[None, None, :, None], held[:, None], 0), axis=2)
    chunks = (count + CHUNK - 1) // CHUNK
    start = jnp.sum(jnp.where(slot[None, None, :] < slot[None, :, None], chunks[:, None, :], 0), axis=2)
    spot = jnp.where(hit, start[:, None, :] * CHUNK + rank, -1).reshape(2, 1, NNZ * NNZ)
    chosen = spot == jnp.arange(ENTRIES, dtype=jnp.int32)[None, :, None]
    left_at = jnp.where(slot == 0, 0, jnp.where(slot < 3, KEPT - 1 + slot, slot - 2))
    both = jnp.broadcast_to(left_at[None, :, None] - NNZ, found.shape) + place * 32
    both = jnp.sum(jnp.where(chosen, both.reshape(2, 1, NNZ * NNZ) + NNZ, 0), axis=2)
    slots = jnp.where(jnp.any(chosen, axis=2), both % 32, NNZ)
    places = both // 32
    c = jnp.arange(ENTRIES // CHUNK, dtype=jnp.int32)[None, :, None]
    chunk_s = jnp.sum((c >= (start + chunks)[:, None, :]).astype(jnp.int32), axis=2)
    steps = (jnp.sum(chunks, axis=1, keepdims=True) + STEP - 1) // STEP
    return steps, chunk_s, slots, places


def on_device(pattern, density, hamiltonian):
    g, d = lax.axis_index("grp"), lax.axis_index("dom")
    odd = g // 2 % 2
    u = jnp.where(odd == 1, d // 4, d % 4)
    own = g % 2 == u // 2
    work_g = jnp.where(own, g, g + 1 - 2 * (g % 2))
    work_d = jnp.where(own, d, d + jnp.where(odd == 1, 4, 1) * (3 - 2 * u))
    lists = tables(pattern, work_g, work_d)
    everything = gather(density, hamiltonian)
    pairs = []
    for gg in range(8):
        for dd in range(16):
            uu, unit = (dd // 4, 4) if gg // 2 % 2 else (dd % 4, 1)
            if gg % 2 != uu // 2:
                pairs.append((gg * 16 + dd, (gg ^ 1) * 16 + dd + unit * (3 - 2 * uu)))
    outs, back, mine = (), [], []
    for w in range(2):
        mine.append(jnp.stack([(work_d * 2 + w) * KEPT, jnp.int32(EXTRA + 2 * w), own.astype(jnp.int32)]))
        *outs, send = one_row(w, *(v[w] for v in lists), mine[w], everything, *outs)
        back.append(lax.ppermute(send, ("grp", "dom"), pairs))
    for w in range(2):
        outs = finish(w, mine[w], back[w], *outs)
    return tuple(outs)


def solution(mesh):
    split = P(("grp", "dom"), None, None, None)
    return jax.shard_map(
        on_device,
        mesh=mesh,
        in_specs=(P(), split, split),
        out_specs=(split, split),
        check_vma=False,
    )
```

```python
import functools

import jax
import jax.numpy as jnp
from jax import lax
from jax.experimental import pallas as pl
from jax.experimental.pallas import tpu as pltpu
from jax.sharding import PartitionSpec as P

MESH = pl.DeviceIdType.MESH
BLK = 128
NNZ = 16
KEPT = 14
SPAN = 32
GROUPS = 8
EXTRA = SPAN * KEPT
TOTAL = EXTRA + 4 + 6 + 6
CHUNK = 2
STEP = 8
ENTRIES = NNZ * NNZ
CUT = {"O": 7, "Q": 4}
PARTS = ((CUT["Q"] + 2, NNZ, CUT["Q"]), (0, 1, 0), (3, CUT["Q"] + 2, 1))

EVENTS = {
    "SZ": ("Z", "u", "v", "single"),
    "PZ": ("Z", "u", "v", "pair"),
    "FZ": ("Z", "u", "vs", "pair"),
    "C0": ("Z", "u", "v", "cross"),
    "Cs": ("Z", "u", "vs", "cross"),
    "Cp": ("Z", "u", "vp", "cross"),
    "Cf": ("Z", "u", "vf", "cross"),
    "Y": ("Y", "u", "v", "cross"),
    "SY": ("Y", "u", "v", "single"),
    "FY": ("Y", "u", "vs", "pair"),
    "SX": ("Y", "un", "v", "single"),
    "FX": ("Y", "un", "vs", "pair"),
}
DETOURS = {"PY": "u", "PX": "un"}
NAMES = tuple(EVENTS) + tuple(n + h for n in DETOURS for h in "123")
N_EV = len(NAMES)
RELAY = {}
LONG = TOTAL
for _hop in "12":
    for _name in DETOURS:
        for _kind in "OQ":
            RELAY[_name + _hop, _kind] = LONG
            LONG += KEPT - CUT[_kind]
ORDER = (
    "S Y O", "S PY1 O", "S C0 O", "S SZ O", "S PZ O", "R SZ O", "R PZ O", "S FZ O",
    "S SY O", "QY", "S Y Q", "R SY O", "S SY Q", "R PY1 O", "R Y O", "QZ",
    "S PY2 O", "S PX1 O", "S FY O", "S PY1 Q", "R PX1 O", "R C0 O", "S PX2 O", "S SX O",
    "S Cp O", "S PZ Q", "R Y Q", "R SY Q", "R PY2 O", "S C0 Q", "S SZ Q", "R PY1 Q",
    "S PY3 O", "R FZ O", "S PX1 Q", "S PY2 Q", "S FY Q", "S Cf O", "R PX2 O", "R FY O",
    "S Cs O", "S PX3 O", "R PY3 O", "R SZ Q", "R SX O", "S Cs Q", "R PX1 Q", "S FZ Q",
    "R FY Q", "S PX2 Q", "R PZ Q", "S FX O", "S SX Q", "R FZ Q", "R PY2 Q", "S PY3 Q",
    "S Cf Q", "R SX Q", "S FX Q", "R Cf O", "R PX2 Q", "R FX O", "S PX3 Q", "R C0 Q",
    "S Cp Q", "R PY3 Q", "SIDES", "R FX Q", "R Cf Q", "R PX3 O", "R Cs Q", "R Cs O",
    "R Cp Q", "R Cp O", "R PX3 Q",
)


def gather_kernel(
    p_ref, h_ref, all_ref,
    ss, rs, ds, dr, loc, ins, inr, qs, qr, es, er, xs, xr,
):
    args = (p_ref, h_ref)
    g, d = lax.axis_index("grp"), lax.axis_index("dom")
    x, c = g // 2, g % 2
    z, y = d // 4, d % 4
    odd = x % 2
    u, v = y + odd * (z - y), z + odd * (y - z)
    host = u // 2
    near = {"u": u, "un": u + 1 - 2 * (u % 2)}
    far = v + 1 - 2 * (v % 2)
    ring = {"v": v, "vs": far, "vp": 3 - v, "vf": (3 - v) + 1 - 2 * ((3 - v) % 2)}

    def dom(uu, vv, swap=odd):
        return vv * 4 + uu + swap * 3 * (uu - vv)

    dq = dom(3 - u, v)
    sib_g = g + 1 - 2 * c
    sibling = (sib_g, d)
    aside, back = (g + GROUPS + 2 - 4 * c) % GROUPS, (g + GROUPS - 2 + 4 * c) % GROUPS
    ways = {
        "single": (g, dom(u, far)),
        "pair": (g, dom(u, 3 - v)),
        "cross": (g, dom(near["un"], v)),
        "1": (aside, d),
        "2": (g, dq),
        "3": (back, d),
    }
    is_own = (c + host + 1) % 2
    work_g = is_own * g + (1 - is_own) * sib_g
    work_d = is_own * d + (1 - is_own) * dq

    def worker(to):
        turned = (to // 2) % 2
        across = y + turned * (z - y)
        same = (across // 2 + to + 1) % 2
        there = d + (1 - turned) * (3 - 2 * y) + turned * 4 * (3 - 2 * z)
        return (
            same * to + (1 - same) * (to + 1 - 2 * (to % 2)),
            same * d + (1 - same) * there,
        )

    up_t, down_t = worker((g + 1) % GROUPS), worker((g + GROUPS - 1) % GROUPS)
    partner_idle = (2 * x + host, dq)

    barrier = pltpu.get_barrier_semaphore()
    for who in (
        *ways.values(), sibling, partner_idle,
        ((work_g + GROUPS - 1) % GROUPS, work_d), ((work_g + 1) % GROUPS, work_d),
    ):
        pl.semaphore_signal(barrier, inc=1, device_id=who, device_id_type=MESH)
    pl.semaphore_wait(barrier, 11 - 2 * is_own)

    def at(dom, row, lo, n):
        return all_ref.at[pl.ds((dom * 2 + row) * KEPT + lo, n)]

    def at1(dom, row, lo, n, a):
        return all_ref.at[pl.ds((dom * 2 + row) * KEPT + lo, n), a]

    def remote(src, dst, s, r, who):
        return pltpu.make_async_remote_copy(
            src_ref=src, dst_ref=dst, send_sem=s, recv_sem=r, device_id=who, device_id_type=MESH
        )

    def init_copies(row, to):
        out = []
        for k, (s0, s1, b) in enumerate(PARTS):
            for a in range(2):
                src = args[a].at[row, pl.ds(s0, s1 - s0)]
                dst = at1(d, row, b, s1 - s0, a)
                if to == "own":
                    out.append(pltpu.make_async_copy(src, dst, loc.at[row, k, a]))
                elif to == "sibling":
                    out.append(remote(src, dst, ins.at[row, k, a], inr.at[row, k, a], sibling))
                else:
                    out.append(remote(src, dst, qs.at[row, k, a], qr.at[k, a], (2 * x + row, dq)))
        return out

    def extra_copies(to):
        out = []
        for row in range(2):
            for a in range(2):
                src = args[a].at[row, pl.ds(1, 2)]
                dst = all_ref.at[pl.ds(EXTRA + 2 * row, 2), a]
                if to == "own":
                    out.append(pltpu.make_async_copy(src, dst, es.at[row, a]))
                else:
                    out.append(remote(src, dst, es.at[row, a], er.at[row, a], (sib_g, dq)))
        return out

    def side_copies():
        out = []
        for k, who, parts in ((0, up_t, ((0, 1), (2, 1))), (1, down_t, ((0, 2),))):
            for row in range(2):
                for a in range(2):
                    for q, (first, n) in enumerate(parts):
                        src = args[a].at[row, pl.ds(first, n)]
                        dst = all_ref.at[pl.ds(EXTRA + 4 + 6 * k + 3 * row + first, n), a]
                        out.append(remote(src, dst, xs.at[2 * k + q, row, a], xr.at[2 * k + q, row, a], who))
        return out

    own = c == host
    for core in range(2):

        @pl.when(jnp.logical_and(own, c == core))
        def _():
            mine = init_copies(core, "own")
            theirs = init_copies(1 - core, "sibling")
            for m, t in zip(mine, theirs):
                m.start()
                t.start()
            for copy in init_copies(core, "sibling") + init_copies(1 - core, "own"):
                copy.start()
            for copy in mine:
                copy.wait()

        @pl.when(jnp.logical_and(jnp.logical_not(own), c == core))
        def _():
            for m, t in zip(init_copies(0, "partner"), init_copies(1, "partner")):
                m.start()
                t.start()
            for copy in init_copies(core, "sibling"):
                copy.wait_recv()

    def turn(uu, kind):
        return uu if kind == "O" else 3 - uu

    seen_by = {
        "single": {"v": "vs"},
        "pair": {"v": "vp", "vs": "vf"},
        "cross": {"v": "v", "vs": "vs", "vp": "vp", "vf": "vf"},
    }

    def event(name, kind, side):
        k = NAMES.index(name) + (N_EV if kind == "Q" else 0)
        cut = CUT[kind]
        n = KEPT - cut
        if name in EVENTS:
            part, col, place, way = EVENTS[name]
            if side == "R":
                place = seen_by[way][place]
                if way == "cross":
                    col = "un"
            lo, n = (0, cut) if part == "Z" else (cut, n)
            owner = dom(turn(near[col], kind), ring[place])
            src = dst = at(owner, c, lo, n)
            what = (owner, lo, n, k)
        else:
            way, base = name[2], name[:2]
            col = DETOURS[base]
            what = None
            relay = {h: all_ref.at[pl.ds(RELAY[base + h, kind], n)] for h in "12"}
            if way == "3" and side == "R":
                owner = dom(turn(near[col], kind), 3 - v)
                src = dst = at(owner, c, cut, n)
                what = (owner, cut, n, k)
            elif way == "3":
                owner = dom(turn({"u": v, "un": far}[col], kind), 3 - u, 1 - odd)
                src, dst = relay["2"], at(owner, c, cut, n)
            elif way == "2":
                src, dst = relay["1"], relay["2"]
            else:
                src, dst = at(dom(turn(near[col], kind), v), c, cut, n), relay["1"]
        return remote(src, dst, ss.at[k], rs.at[k], ways[way]), what

    passed = []

    def to_sibling(dom, lo, n, k):
        ref = at(dom, c, lo, n)
        remote(ref, ref, ds.at[k], dr.at[k], sibling).start()
        passed.append((dom, lo, n, k))

    sent = []

    def send(name, kind):
        copy, _ = event(name, kind, "S")
        copy.start()
        sent.append(copy)

    def receive(name, kind):
        copy, what = event(name, kind, "R")
        copy.wait_recv()
        if what is not None:
            to_sibling(*what)

    def receive_partner(parts, lo, n, k):
        for part in parts:
            s0, s1, b = PARTS[part]
            for a in range(2):
                ref = at1(dq, c, b, s1 - s0, a)
                remote(ref, ref, qs.at[0, part, a], qr.at[part, a], sibling).wait_recv()
        to_sibling(dq, lo, n, k)

    sides = side_copies()

    def start_sides():
        for copy in sides:
            copy.start()

        @pl.when(own)
        def _():
            for copy in extra_copies("own"):
                copy.start()

        @pl.when(jnp.logical_not(own))
        def _():
            for copy in extra_copies("partner"):
                copy.start()

    for step in ORDER:
        if step == "SIDES":
            start_sides()
        elif step == "QY":
            receive_partner((0,), CUT["Q"], KEPT - CUT["Q"], 2 * N_EV)
        elif step == "QZ":
            receive_partner((1, 2), 0, CUT["Q"], 2 * N_EV + 1)
        else:
            what, name, kind = step.split()
            (send if what == "S" else receive)(name, kind)

    for core in range(2):

        @pl.when(jnp.logical_and(own, c == core))
        def _():
            for copy in init_copies(1 - core, "own") + extra_copies("own"):
                copy.wait()
            for copy in init_copies(0, "sibling") + init_copies(1, "sibling"):
                copy.wait_send()

        @pl.when(jnp.logical_and(jnp.logical_not(own), c == core))
        def _():
            for copy in init_copies(1 - core, "sibling"):
                copy.wait_recv()
            for copy in init_copies(0, "partner") + init_copies(1, "partner"):
                copy.wait_send()
            for copy in extra_copies("partner"):
                copy.wait()

    for copy in sides:
        copy.wait()
    for copy in sent:
        copy.wait_send()
    for dom, lo, n, k in passed:
        mine, theirs = at(dom, c, lo, n), at(dom, 1 - c, lo, n)
        remote(mine, mine, ds.at[k], dr.at[k], sibling).wait_send()
        remote(theirs, theirs, ds.at[k], dr.at[k], sibling).wait_recv()


def gather(density, hamiltonian):
    dma = pltpu.SemaphoreType.DMA
    return pl.pallas_call(
        gather_kernel,
        name="gather",
        out_shape=jax.ShapeDtypeStruct((LONG, 2, BLK, BLK), jnp.bfloat16),
        in_specs=[pl.BlockSpec(memory_space=pltpu.VMEM)] * 2,
        out_specs=pl.BlockSpec(memory_space=pl.ANY),
        scratch_shapes=[
            dma((2 * N_EV,)), dma((2 * N_EV,)), dma((2 * N_EV + 2,)), dma((2 * N_EV + 2,)),
            dma((2, 3, 2)), dma((2, 3, 2)), dma((2, 3, 2)), dma((2, 3, 2)), dma((3, 2)),
            dma((2, 2)), dma((2, 2)), dma((3, 2, 2)), dma((3, 2, 2)),
        ],
        compiler_params=pltpu.CompilerParams(collective_id=0, has_side_effects=True),
    )(density, hamiltonian)


def row_kernel(
    steps, chunk_s, slots, places, mine, all_ref, x_ref, g_ref, send_ref,
    left, right, low, high, mid, sem_a, sem_b,
):
    def fetch_left(lo, n, at):
        return pltpu.make_async_copy(
            all_ref.at[pl.ds(at, n)], left.at[pl.ds(lo, n)], sem_a.at[lo // KEPT]
        )

    def fetch(e):
        return pltpu.make_async_copy(all_ref.at[places[e]], right.at[e], sem_b.at[e])

    def fetch_step(q, what):
        for k in range(STEP * CHUNK):
            what(fetch(q * (STEP * CHUNK) + k))

    a_copies = (fetch_left(0, KEPT, mine[0]), fetch_left(KEPT, 2, mine[1]))
    for copy in a_copies:
        copy.start()

    @pl.loop(0, steps[0])
    def _(q):
        fetch_step(q, lambda copy: copy.start())

    left[NNZ] = jnp.zeros((2, BLK, BLK), jnp.bfloat16)
    mid[NNZ] = jnp.zeros((2, BLK, BLK), jnp.bfloat16)
    for s in range(NNZ):
        low[s] = jnp.zeros((BLK, 2 * BLK), jnp.float32)
        high[s] = jnp.zeros((BLK, 2 * BLK), jnp.float32)
    for copy in a_copies:
        copy.wait()

    def step(q, a_ref, total):
        sums = []
        for k in range(STEP):
            first = (q * STEP + k) * CHUNK
            e = [first + p for p in range(CHUNK)]
            t = [slots[p] for p in e]
            a = jnp.concatenate([a_ref[p, 0] for p in t], axis=1)
            b = jnp.concatenate([a_ref[p, 1] for p in t], axis=1)
            den = jnp.concatenate([right[p, 0] for p in e], axis=0)
            ham = jnp.concatenate([right[p, 1] for p in e], axis=0)
            both = jnp.dot(a, jnp.concatenate([den, ham], axis=1), preferred_element_type=jnp.float32)
            more = jnp.dot(b, den, preferred_element_type=jnp.float32)
            sums.append((both, more))
        for k in range(STEP):
            s = chunk_s[q * STEP + k]
            both, more = sums[k]
            total[s, :, :BLK] += both[:, :BLK]
            total[s, :, BLK:] += both[:, BLK:] + more

    @pl.loop(0, steps[0])
    def _(q):
        fetch_step(q, lambda copy: copy.wait())
        step(q, left, low)

    for s in range(NNZ):
        at = 0 if s == 0 else KEPT - 1 + s if s < 3 else s - 2
        mid[at, 0] = low[s, :, :BLK].astype(jnp.bfloat16)
        mid[at, 1] = low[s, :, BLK:].astype(jnp.bfloat16)

    @pl.loop(0, steps[0])
    def _(q):
        step(q, mid, high)

    for s in range(NNZ):
        purified = 3.0 * low[s, :, :BLK] - 2.0 * high[s, :, :BLK]
        gradient = 3.0 * low[s, :, BLK:] - 2.0 * high[s, :, BLK:]
        x_ref[s] = purified
        g_ref[s] = gradient
        send_ref[0, s] = purified.astype(jnp.bfloat16)
        send_ref[1, s] = gradient.astype(jnp.bfloat16)


def one_row(name, steps, chunk_s, slots, places, mine, everything):
    f32, bf16 = jnp.float32, jnp.bfloat16
    vmem = pl.BlockSpec(memory_space=pltpu.VMEM)
    smem = pl.BlockSpec(memory_space=pltpu.SMEM)
    return pl.pallas_call(
        row_kernel,
        name=name,
        out_shape=(
            jax.ShapeDtypeStruct((NNZ, BLK, BLK), f32),
            jax.ShapeDtypeStruct((NNZ, BLK, BLK), f32),
            jax.ShapeDtypeStruct((2, NNZ, BLK, BLK), bf16),
        ),
        in_specs=[smem] * 5 + [pl.BlockSpec(memory_space=pl.ANY)],
        out_specs=(vmem, vmem, vmem),
        scratch_shapes=[
            pltpu.VMEM((NNZ + 1, 2, BLK, BLK), bf16),
            pltpu.VMEM((ENTRIES, 2, BLK, BLK), bf16),
            pltpu.VMEM((NNZ + 1, BLK, 2 * BLK), f32),
            pltpu.VMEM((NNZ + 1, BLK, 2 * BLK), f32),
            pltpu.VMEM((NNZ + 1, 2, BLK, BLK), bf16),
            pltpu.SemaphoreType.DMA((2,)),
            pltpu.SemaphoreType.DMA((ENTRIES,)),
        ],
        compiler_params=pltpu.CompilerParams(vmem_limit_bytes=40 << 20),
        cost_estimate=pl.CostEstimate(
            flops=2 * 2 * 3 * 104 * BLK**3, bytes_accessed=14 << 20, transcendentals=0
        ),
    )(steps, chunk_s, slots, places, mine, everything)


def tables(pattern, work_g, work_d):
    first = work_g * SPAN + work_d * 2
    cols = lax.dynamic_slice_in_dim(pattern, first, 2, 0)
    far = jnp.take(pattern, cols, axis=0)
    slot = jnp.arange(NNZ, dtype=jnp.int32)
    found = jnp.max(
        jnp.where(far[:, :, None, :] == cols[:, None, :, None], slot + 1, 0), axis=3
    ) - 1
    group, inner = cols // SPAN, cols % SPAN
    row = cols % 2
    inside = (group == work_g)[:, :, None]
    before = (group == (work_g + GROUPS - 1) % GROUPS)[:, :, None]
    short = jnp.clip(found, 0, 2)
    place = jnp.where(
        inside,
        jnp.where(
            (found == 1) | (found == 2),
            EXTRA + 2 * row[:, :, None] + jnp.clip(found - 1, 0, 1),
            inner[:, :, None] * KEPT + jnp.where(found < 3, 0, found - 2),
        ),
        EXTRA + 4 + 3 * row[:, :, None] + short + jnp.where(before, 0, 6),
    )
    hit = found >= 0
    held = hit.astype(jnp.int32)
    count = jnp.sum(held, axis=1)
    rank = jnp.sum(jnp.where(slot[None, :, None, None] > slot[None, None, :, None], held[:, None], 0), axis=2)
    chunks = (count + CHUNK - 1) // CHUNK
    start = jnp.sum(jnp.where(slot[None, None, :] < slot[None, :, None], chunks[:, None, :], 0), axis=2)
    spot = jnp.where(hit, start[:, None, :] * CHUNK + rank, -1).reshape(2, 1, NNZ * NNZ)
    chosen = spot == jnp.arange(ENTRIES, dtype=jnp.int32)[None, :, None]
    left_at = jnp.where(slot == 0, 0, jnp.where(slot < 3, KEPT - 1 + slot, slot - 2))
    both = jnp.broadcast_to(left_at[None, :, None] - NNZ, found.shape) + place * 32
    both = jnp.sum(jnp.where(chosen, both.reshape(2, 1, NNZ * NNZ) + NNZ, 0), axis=2)
    slots = jnp.where(jnp.any(chosen, axis=2), both % 32, NNZ)
    places = both // 32
    c = jnp.arange(ENTRIES // CHUNK, dtype=jnp.int32)[None, :, None]
    chunk_s = jnp.sum((c >= (start + chunks)[:, None, :]).astype(jnp.int32), axis=2)
    steps = (jnp.sum(chunks, axis=1, keepdims=True) + STEP - 1) // STEP
    return steps, chunk_s, slots, places


def on_device(pattern, density, hamiltonian):
    g, d = lax.axis_index("grp"), lax.axis_index("dom")
    odd = g // 2 % 2
    u = jnp.where(odd == 1, d // 4, d % 4)
    own = g % 2 == u // 2
    work_g = jnp.where(own, g, g + 1 - 2 * (g % 2))
    work_d = jnp.where(own, d, d + jnp.where(odd == 1, 4, 1) * (3 - 2 * u))
    lists = tables(pattern, work_g, work_d)
    everything = gather(density, hamiltonian)
    pairs = []
    for gg in range(8):
        for dd in range(16):
            uu, unit = (dd // 4, 4) if gg // 2 % 2 else (dd % 4, 1)
            if gg % 2 != uu // 2:
                pairs.append((gg * 16 + dd, (gg ^ 1) * 16 + dd + unit * (3 - 2 * uu)))
    mine, back = [], []
    for w in range(2):
        where = jnp.stack([(work_d * 2 + w) * KEPT, jnp.int32(EXTRA + 2 * w)])
        px, gx, out = one_row(f"row{w}", *(v[w] for v in lists), where, everything)
        mine.append((px, gx))
        back.append(lax.ppermute(out, ("grp", "dom"), pairs))
    res = []
    for k in range(2):
        res.append(jnp.stack([
            jnp.where(own, mine[w][k], back[w][k].astype(jnp.float32)) for w in range(2)
        ]))
    return tuple(res)


def solution(mesh):
    split = P(("grp", "dom"), None, None, None)
    return jax.shard_map(
        on_device,
        mesh=mesh,
        in_specs=(P(), split, split),
        out_specs=(split, split),
        check_vma=False,
    )
```

```python
import functools

import jax
import jax.numpy as jnp
from jax import lax
from jax.experimental import pallas as pl
from jax.experimental.pallas import tpu as pltpu
from jax.sharding import PartitionSpec as P

MESH = pl.DeviceIdType.MESH
BLK = 128
NNZ = 16
KEPT = 14
SPAN = 32
GROUPS = 8
EXTRA = SPAN * KEPT
TOTAL = EXTRA + 4 + 6 + 6
CHUNK = 2
STEP = 8
ENTRIES = NNZ * NNZ
WHERE = 2 * ENTRIES + ENTRIES // CHUNK
CUT = {"O": 7, "Q": 4}
PARTS = ((CUT["Q"] + 2, NNZ, CUT["Q"]), (0, 1, 0), (3, CUT["Q"] + 2, 1))

EVENTS = {
    "SZ": ("Z", "u", "v", "single"),
    "PZ": ("Z", "u", "v", "pair"),
    "FZ": ("Z", "u", "vs", "pair"),
    "C0": ("Z", "u", "v", "cross"),
    "Cs": ("Z", "u", "vs", "cross"),
    "Cp": ("Z", "u", "vp", "cross"),
    "Cf": ("Z", "u", "vf", "cross"),
    "Y": ("Y", "u", "v", "cross"),
    "SY": ("Y", "u", "v", "single"),
    "FY": ("Y", "u", "vs", "pair"),
    "SX": ("Y", "un", "v", "single"),
    "FX": ("Y", "un", "vs", "pair"),
}
DETOURS = {"PY": "u", "PX": "un"}
NAMES = tuple(EVENTS) + tuple(n + h for n in DETOURS for h in "123")
N_EV = len(NAMES)
RELAY = {}
LONG = TOTAL
for _hop in "12":
    for _name in DETOURS:
        for _kind in "OQ":
            RELAY[_name + _hop, _kind] = LONG
            LONG += KEPT - CUT[_kind]
ORDER = (
    "S Y O", "S PY1 O", "S C0 O", "S SZ O", "S PZ O", "R SZ O", "R PZ O", "S FZ O",
    "S SY O", "QY", "S Y Q", "R SY O", "S SY Q", "R PY1 O", "R Y O", "QZ",
    "S PY2 O", "S PX1 O", "S FY O", "S PY1 Q", "R PX1 O", "R C0 O", "S PX2 O", "S SX O",
    "S Cp O", "S PZ Q", "R Y Q", "R SY Q", "R PY2 O", "S C0 Q", "S SZ Q", "R PY1 Q",
    "S PY3 O", "R FZ O", "S PX1 Q", "S PY2 Q", "S FY Q", "S Cf O", "R PX2 O", "R FY O",
    "S Cs O", "S PX3 O", "R PY3 O", "R SZ Q", "R SX O", "S Cs Q", "R PX1 Q", "S FZ Q",
    "R FY Q", "S PX2 Q", "R PZ Q", "S FX O", "S SX Q", "R FZ Q", "R PY2 Q", "S PY3 Q",
    "S Cf Q", "R SX Q", "S FX Q", "R Cf O", "R PX2 Q", "R FX O", "S PX3 Q", "R C0 Q",
    "S Cp Q", "R PY3 Q", "SIDES", "R FX Q", "R Cf Q", "R PX3 O", "R Cs Q", "R Cs O",
    "R Cp Q", "R Cp O", "R PX3 Q",
)


def gather_kernel(
    p_ref, h_ref, all_ref,
    ss, rs, ds, dr, loc, ins, inr, qs, qr, es, er, xs, xr,
):
    args = (p_ref, h_ref)
    g, d = lax.axis_index("grp"), lax.axis_index("dom")
    x, c = g // 2, g % 2
    z, y = d // 4, d % 4
    odd = x % 2
    u, v = y + odd * (z - y), z + odd * (y - z)
    host = u // 2
    near = {"u": u, "un": u + 1 - 2 * (u % 2)}
    far = v + 1 - 2 * (v % 2)
    ring = {"v": v, "vs": far, "vp": 3 - v, "vf": (3 - v) + 1 - 2 * ((3 - v) % 2)}

    def dom(uu, vv, swap=odd):
        return vv * 4 + uu + swap * 3 * (uu - vv)

    dq = dom(3 - u, v)
    sib_g = g + 1 - 2 * c
    sibling = (sib_g, d)
    aside, back = (g + GROUPS + 2 - 4 * c) % GROUPS, (g + GROUPS - 2 + 4 * c) % GROUPS
    ways = {
        "single": (g, dom(u, far)),
        "pair": (g, dom(u, 3 - v)),
        "cross": (g, dom(near["un"], v)),
        "1": (aside, d),
        "2": (g, dq),
        "3": (back, d),
    }
    is_own = (c + host + 1) % 2
    work_g = is_own * g + (1 - is_own) * sib_g
    work_d = is_own * d + (1 - is_own) * dq

    def worker(to):
        turned = (to // 2) % 2
        across = y + turned * (z - y)
        same = (across // 2 + to + 1) % 2
        there = d + (1 - turned) * (3 - 2 * y) + turned * 4 * (3 - 2 * z)
        return (
            same * to + (1 - same) * (to + 1 - 2 * (to % 2)),
            same * d + (1 - same) * there,
        )

    up_t, down_t = worker((g + 1) % GROUPS), worker((g + GROUPS - 1) % GROUPS)
    partner_idle = (2 * x + host, dq)

    barrier = pltpu.get_barrier_semaphore()
    for who in (
        *ways.values(), sibling, partner_idle,
        ((work_g + GROUPS - 1) % GROUPS, work_d), ((work_g + 1) % GROUPS, work_d),
    ):
        pl.semaphore_signal(barrier, inc=1, device_id=who, device_id_type=MESH)
    pl.semaphore_wait(barrier, 11 - 2 * is_own)

    def at(dom, row, lo, n):
        return all_ref.at[pl.ds((dom * 2 + row) * KEPT + lo, n)]

    def at1(dom, row, lo, n, a):
        return all_ref.at[pl.ds((dom * 2 + row) * KEPT + lo, n), a]

    def remote(src, dst, s, r, who):
        return pltpu.make_async_remote_copy(
            src_ref=src, dst_ref=dst, send_sem=s, recv_sem=r, device_id=who, device_id_type=MESH
        )

    def init_copies(row, to):
        out = []
        for k, (s0, s1, b) in enumerate(PARTS):
            for a in range(2):
                src = args[a].at[row, pl.ds(s0, s1 - s0)]
                dst = at1(d, row, b, s1 - s0, a)
                if to == "own":
                    out.append(pltpu.make_async_copy(src, dst, loc.at[row, k, a]))
                elif to == "sibling":
                    out.append(remote(src, dst, ins.at[row, k, a], inr.at[row, k, a], sibling))
                else:
                    out.append(remote(src, dst, qs.at[row, k, a], qr.at[k, a], (2 * x + row, dq)))
        return out

    def extra_copies(to):
        out = []
        for row in range(2):
            for a in range(2):
                src = args[a].at[row, pl.ds(1, 2)]
                dst = all_ref.at[pl.ds(EXTRA + 2 * row, 2), a]
                if to == "own":
                    out.append(pltpu.make_async_copy(src, dst, es.at[row, a]))
                else:
                    out.append(remote(src, dst, es.at[row, a], er.at[row, a], (sib_g, dq)))
        return out

    def side_copies():
        out = []
        for k, who, parts in ((0, up_t, ((0, 1), (2, 1))), (1, down_t, ((0, 2),))):
            for row in range(2):
                for a in range(2):
                    for q, (first, n) in enumerate(parts):
                        src = args[a].at[row, pl.ds(first, n)]
                        dst = all_ref.at[pl.ds(EXTRA + 4 + 6 * k + 3 * row + first, n), a]
                        out.append(remote(src, dst, xs.at[2 * k + q, row, a], xr.at[2 * k + q, row, a], who))
        return out

    own = c == host
    for core in range(2):

        @pl.when(jnp.logical_and(own, c == core))
        def _():
            mine = init_copies(core, "own")
            theirs = init_copies(1 - core, "sibling")
            for m, t in zip(mine, theirs):
                m.start()
                t.start()
            for copy in init_copies(core, "sibling") + init_copies(1 - core, "own"):
                copy.start()
            for copy in mine:
                copy.wait()

        @pl.when(jnp.logical_and(jnp.logical_not(own), c == core))
        def _():
            for m, t in zip(init_copies(0, "partner"), init_copies(1, "partner")):
                m.start()
                t.start()
            for copy in init_copies(core, "sibling"):
                copy.wait_recv()

    def turn(uu, kind):
        return uu if kind == "O" else 3 - uu

    seen_by = {
        "single": {"v": "vs"},
        "pair": {"v": "vp", "vs": "vf"},
        "cross": {"v": "v", "vs": "vs", "vp": "vp", "vf": "vf"},
    }

    def event(name, kind, side):
        k = NAMES.index(name) + (N_EV if kind == "Q" else 0)
        cut = CUT[kind]
        n = KEPT - cut
        if name in EVENTS:
            part, col, place, way = EVENTS[name]
            if side == "R":
                place = seen_by[way][place]
                if way == "cross":
                    col = "un"
            lo, n = (0, cut) if part == "Z" else (cut, n)
            owner = dom(turn(near[col], kind), ring[place])
            src = dst = at(owner, c, lo, n)
            what = (owner, lo, n, k)
        else:
            way, base = name[2], name[:2]
            col = DETOURS[base]
            what = None
            relay = {h: all_ref.at[pl.ds(RELAY[base + h, kind], n)] for h in "12"}
            if way == "3" and side == "R":
                owner = dom(turn(near[col], kind), 3 - v)
                src = dst = at(owner, c, cut, n)
                what = (owner, cut, n, k)
            elif way == "3":
                owner = dom(turn({"u": v, "un": far}[col], kind), 3 - u, 1 - odd)
                src, dst = relay["2"], at(owner, c, cut, n)
            elif way == "2":
                src, dst = relay["1"], relay["2"]
            else:
                src, dst = at(dom(turn(near[col], kind), v), c, cut, n), relay["1"]
        return remote(src, dst, ss.at[k], rs.at[k], ways[way]), what

    passed = []

    def to_sibling(dom, lo, n, k):
        ref = at(dom, c, lo, n)
        remote(ref, ref, ds.at[k], dr.at[k], sibling).start()
        passed.append((dom, lo, n, k))

    sent = []

    def send(name, kind):
        copy, _ = event(name, kind, "S")
        copy.start()
        sent.append(copy)

    def receive(name, kind):
        copy, what = event(name, kind, "R")
        copy.wait_recv()
        if what is not None:
            to_sibling(*what)

    def receive_partner(parts, lo, n, k):
        for part in parts:
            s0, s1, b = PARTS[part]
            for a in range(2):
                ref = at1(dq, c, b, s1 - s0, a)
                remote(ref, ref, qs.at[0, part, a], qr.at[part, a], sibling).wait_recv()
        to_sibling(dq, lo, n, k)

    sides = side_copies()

    def start_sides():
        for copy in sides:
            copy.start()

        @pl.when(own)
        def _():
            for copy in extra_copies("own"):
                copy.start()

        @pl.when(jnp.logical_not(own))
        def _():
            for copy in extra_copies("partner"):
                copy.start()

    for step in ORDER:
        if step == "SIDES":
            start_sides()
        elif step == "QY":
            receive_partner((0,), CUT["Q"], KEPT - CUT["Q"], 2 * N_EV)
        elif step == "QZ":
            receive_partner((1, 2), 0, CUT["Q"], 2 * N_EV + 1)
        else:
            what, name, kind = step.split()
            (send if what == "S" else receive)(name, kind)

    for core in range(2):

        @pl.when(jnp.logical_and(own, c == core))
        def _():
            for copy in init_copies(1 - core, "own") + extra_copies("own"):
                copy.wait()
            for copy in init_copies(0, "sibling") + init_copies(1, "sibling"):
                copy.wait_send()

        @pl.when(jnp.logical_and(jnp.logical_not(own), c == core))
        def _():
            for copy in init_copies(1 - core, "sibling"):
                copy.wait_recv()
            for copy in init_copies(0, "partner") + init_copies(1, "partner"):
                copy.wait_send()
            for copy in extra_copies("partner"):
                copy.wait()

    for copy in sides:
        copy.wait()
    for copy in sent:
        copy.wait_send()
    for dom, lo, n, k in passed:
        mine, theirs = at(dom, c, lo, n), at(dom, 1 - c, lo, n)
        remote(mine, mine, ds.at[k], dr.at[k], sibling).wait_send()
        remote(theirs, theirs, ds.at[k], dr.at[k], sibling).wait_recv()


def gather(density, hamiltonian):
    dma = pltpu.SemaphoreType.DMA
    return pl.pallas_call(
        gather_kernel,
        name="gather",
        out_shape=jax.ShapeDtypeStruct((LONG, 2, BLK, BLK), jnp.bfloat16),
        in_specs=[pl.BlockSpec(memory_space=pltpu.VMEM)] * 2,
        out_specs=pl.BlockSpec(memory_space=pl.ANY),
        scratch_shapes=[
            dma((2 * N_EV,)), dma((2 * N_EV,)), dma((2 * N_EV + 2,)), dma((2 * N_EV + 2,)),
            dma((2, 3, 2)), dma((2, 3, 2)), dma((2, 3, 2)), dma((2, 3, 2)), dma((3, 2)),
            dma((2, 2)), dma((2, 2)), dma((3, 2, 2)), dma((3, 2, 2)),
        ],
        compiler_params=pltpu.CompilerParams(collective_id=0, has_side_effects=True),
    )(density, hamiltonian)


def row_kernel(
    table, all_ref, x_ref, g_ref, send_ref,
    left, right, low, high, mid, sem_a, sem_b,
):
    def fetch_left(lo, n, at):
        return pltpu.make_async_copy(
            all_ref.at[pl.ds(at, n)], left.at[pl.ds(lo, n)], sem_a.at[lo // KEPT]
        )

    def fetch(e):
        return pltpu.make_async_copy(all_ref.at[table[e]], right.at[e], sem_b.at[e])

    def fetch_step(q, what):
        for k in range(STEP * CHUNK):
            what(fetch(q * (STEP * CHUNK) + k))

    a_copies = (fetch_left(0, KEPT, table[WHERE]), fetch_left(KEPT, 2, table[WHERE + 1]))
    for copy in a_copies:
        copy.start()

    @pl.loop(0, table[WHERE + 2])
    def _(q):
        fetch_step(q, lambda copy: copy.start())

    left[NNZ] = jnp.zeros((2, BLK, BLK), jnp.bfloat16)
    mid[NNZ] = jnp.zeros((2, BLK, BLK), jnp.bfloat16)
    for s in range(NNZ):
        low[s] = jnp.zeros((BLK, 2 * BLK), jnp.float32)
        high[s] = jnp.zeros((BLK, 2 * BLK), jnp.float32)
    for copy in a_copies:
        copy.wait()

    def step(q, a_ref, total):
        sums = []
        for k in range(STEP):
            first = (q * STEP + k) * CHUNK
            e = [first + p for p in range(CHUNK)]
            t = [table[ENTRIES + p] for p in e]
            a = jnp.concatenate([a_ref[p, 0] for p in t], axis=1)
            b = jnp.concatenate([a_ref[p, 1] for p in t], axis=1)
            den = jnp.concatenate([right[p, 0] for p in e], axis=0)
            ham = jnp.concatenate([right[p, 1] for p in e], axis=0)
            both = jnp.dot(a, jnp.concatenate([den, ham], axis=1), preferred_element_type=jnp.float32)
            more = jnp.dot(b, den, preferred_element_type=jnp.float32)
            sums.append((both, more))
        for k in range(STEP):
            s = table[2 * ENTRIES + q * STEP + k]
            both, more = sums[k]
            total[s, :, :BLK] += both[:, :BLK]
            total[s, :, BLK:] += both[:, BLK:] + more

    @pl.loop(0, table[WHERE + 2])
    def _(q):
        fetch_step(q, lambda copy: copy.wait())
        step(q, left, low)

    for s in range(NNZ):
        at = 0 if s == 0 else KEPT - 1 + s if s < 3 else s - 2
        mid[at, 0] = low[s, :, :BLK].astype(jnp.bfloat16)
        mid[at, 1] = low[s, :, BLK:].astype(jnp.bfloat16)

    @pl.loop(0, table[WHERE + 2])
    def _(q):
        step(q, mid, high)

    for s in range(NNZ):
        purified = 3.0 * low[s, :, :BLK] - 2.0 * high[s, :, :BLK]
        gradient = 3.0 * low[s, :, BLK:] - 2.0 * high[s, :, BLK:]
        x_ref[s] = purified
        g_ref[s] = gradient
        send_ref[0, s] = purified.astype(jnp.bfloat16)
        send_ref[1, s] = gradient.astype(jnp.bfloat16)


def one_row(name, table, everything):
    f32, bf16 = jnp.float32, jnp.bfloat16
    vmem = pl.BlockSpec(memory_space=pltpu.VMEM)
    smem = pl.BlockSpec(memory_space=pltpu.SMEM)
    return pl.pallas_call(
        row_kernel,
        name=name,
        out_shape=(
            jax.ShapeDtypeStruct((NNZ, BLK, BLK), f32),
            jax.ShapeDtypeStruct((NNZ, BLK, BLK), f32),
            jax.ShapeDtypeStruct((2, NNZ, BLK, BLK), bf16),
        ),
        in_specs=[smem, pl.BlockSpec(memory_space=pl.ANY)],
        out_specs=(vmem, vmem, vmem),
        scratch_shapes=[
            pltpu.VMEM((NNZ + 1, 2, BLK, BLK), bf16),
            pltpu.VMEM((ENTRIES, 2, BLK, BLK), bf16),
            pltpu.VMEM((NNZ + 1, BLK, 2 * BLK), f32),
            pltpu.VMEM((NNZ + 1, BLK, 2 * BLK), f32),
            pltpu.VMEM((NNZ + 1, 2, BLK, BLK), bf16),
            pltpu.SemaphoreType.DMA((2,)),
            pltpu.SemaphoreType.DMA((ENTRIES,)),
        ],
        compiler_params=pltpu.CompilerParams(vmem_limit_bytes=40 << 20),
        cost_estimate=pl.CostEstimate(
            flops=2 * 2 * 3 * 104 * BLK**3, bytes_accessed=14 << 20, transcendentals=0
        ),
    )(table, everything)


def tables(pattern, work_g, work_d):
    first = work_g * SPAN + work_d * 2
    cols = lax.dynamic_slice_in_dim(pattern, first, 2, 0)
    picks = (cols.reshape(2 * NNZ, 1) == jnp.arange(pattern.shape[0], dtype=jnp.int32)).astype(jnp.bfloat16)
    far = jnp.dot(picks, pattern.astype(jnp.bfloat16), preferred_element_type=jnp.float32)
    far = far.astype(jnp.int32).reshape(2, NNZ, NNZ)
    slot = jnp.arange(NNZ, dtype=jnp.int32)
    found = jnp.max(
        jnp.where(far[:, :, None, :] == cols[:, None, :, None], slot + 1, 0), axis=3
    ) - 1
    group, inner = cols // SPAN, cols % SPAN
    row = cols % 2
    inside = (group == work_g)[:, :, None]
    before = (group == (work_g + GROUPS - 1) % GROUPS)[:, :, None]
    short = jnp.clip(found, 0, 2)
    place = jnp.where(
        inside,
        jnp.where(
            (found == 1) | (found == 2),
            EXTRA + 2 * row[:, :, None] + jnp.clip(found - 1, 0, 1),
            inner[:, :, None] * KEPT + jnp.where(found < 3, 0, found - 2),
        ),
        EXTRA + 4 + 3 * row[:, :, None] + short + jnp.where(before, 0, 6),
    )
    hit = found >= 0
    held = hit.astype(jnp.int32)
    count = jnp.sum(held, axis=1)
    rank = jnp.sum(jnp.where(slot[None, :, None, None] > slot[None, None, :, None], held[:, None], 0), axis=2)
    chunks = (count + CHUNK - 1) // CHUNK
    start = jnp.sum(jnp.where(slot[None, None, :] < slot[None, :, None], chunks[:, None, :], 0), axis=2)
    spot = jnp.where(hit, start[:, None, :] * CHUNK + rank, -1).reshape(2, 1, NNZ * NNZ)
    chosen = spot == jnp.arange(ENTRIES, dtype=jnp.int32)[None, :, None]
    left_at = jnp.where(slot == 0, 0, jnp.where(slot < 3, KEPT - 1 + slot, slot - 2))
    both = jnp.broadcast_to(left_at[None, :, None] - NNZ, found.shape) + place * 32
    both = jnp.sum(jnp.where(chosen, both.reshape(2, 1, NNZ * NNZ) + NNZ, 0), axis=2)
    slots = jnp.where(jnp.any(chosen, axis=2), both % 32, NNZ)
    places = both // 32
    c = jnp.arange(ENTRIES // CHUNK, dtype=jnp.int32)[None, :, None]
    chunk_s = jnp.sum((c >= (start + chunks)[:, None, :]).astype(jnp.int32), axis=2)
    steps = (jnp.sum(chunks, axis=1, keepdims=True) + STEP - 1) // STEP
    row_at = (work_d * 2 + jnp.arange(2, dtype=jnp.int32)[:, None]) * KEPT
    extra_at = EXTRA + 2 * jnp.arange(2, dtype=jnp.int32)[:, None]
    return jnp.concatenate([places, slots, chunk_s, row_at, extra_at, steps], axis=1)


def on_device(pattern, density, hamiltonian):
    g, d = lax.axis_index("grp"), lax.axis_index("dom")
    odd = g // 2 % 2
    u = jnp.where(odd == 1, d // 4, d % 4)
    own = g % 2 == u // 2
    work_g = jnp.where(own, g, g + 1 - 2 * (g % 2))
    work_d = jnp.where(own, d, d + jnp.where(odd == 1, 4, 1) * (3 - 2 * u))
    lists = tables(pattern, work_g, work_d)
    everything = gather(density, hamiltonian)
    pairs = []
    for gg in range(8):
        for dd in range(16):
            uu, unit = (dd // 4, 4) if gg // 2 % 2 else (dd % 4, 1)
            if gg % 2 != uu // 2:
                pairs.append((gg * 16 + dd, (gg ^ 1) * 16 + dd + unit * (3 - 2 * uu)))
    mine, back = [], []
    for w in range(2):
        px, gx, out = one_row(f"row{w}", lists[w], everything)
        mine.append((px, gx))
        back.append(lax.ppermute(out, ("grp", "dom"), pairs))
    res = []
    for k in range(2):
        rows = [jnp.where(own, mine[w][k], back[w][k].astype(jnp.float32))[None] for w in range(2)]
        both = jnp.broadcast_to(rows[0], (2, NNZ, BLK, BLK))
        res.append(lax.dynamic_update_slice(both, rows[1], (1, 0, 0, 0)))
    return tuple(res)


def solution(mesh):
    split = P(("grp", "dom"), None, None, None)
    return jax.shard_map(
        on_device,
        mesh=mesh,
        in_specs=(P(), split, split),
        out_specs=(split, split),
        check_vma=False,
    )
```

```python
import functools

import jax
import jax.numpy as jnp
from jax import lax
from jax.experimental import pallas as pl
from jax.experimental.pallas import tpu as pltpu
from jax.sharding import PartitionSpec as P

MESH = pl.DeviceIdType.MESH
BLK = 128
NNZ = 16
KEPT = 14
SPAN = 32
GROUPS = 8
EXTRA = SPAN * KEPT
TOTAL = EXTRA + 4 + 6 + 6
CHUNK = 2
STEP = 8
ENTRIES = NNZ * NNZ
WHERE = 2 * ENTRIES + ENTRIES // CHUNK
CUT = {"O": 7, "Q": 4}
PARTS = ((CUT["Q"] + 2, NNZ, CUT["Q"]), (0, 1, 0), (3, CUT["Q"] + 2, 1))

EVENTS = {
    "SZ": ("Z", "u", "v", "single"),
    "PZ": ("Z", "u", "v", "pair"),
    "FZ": ("Z", "u", "vs", "pair"),
    "C0": ("Z", "u", "v", "cross"),
    "Cs": ("Z", "u", "vs", "cross"),
    "Cp": ("Z", "u", "vp", "cross"),
    "Cf": ("Z", "u", "vf", "cross"),
    "Y": ("Y", "u", "v", "cross"),
    "SY": ("Y", "u", "v", "single"),
    "FY": ("Y", "u", "vs", "pair"),
    "SX": ("Y", "un", "v", "single"),
    "FX": ("Y", "un", "vs", "pair"),
}
DETOURS = {"PY": "u", "PX": "un"}
NAMES = tuple(EVENTS) + tuple(n + h for n in DETOURS for h in "123")
N_EV = len(NAMES)
RELAY = {}
LONG = TOTAL
for _hop in "12":
    for _name in DETOURS:
        for _kind in "OQ":
            RELAY[_name + _hop, _kind] = LONG
            LONG += KEPT - CUT[_kind]
ORDER = (
    "S Y O", "S PY1 O", "S C0 O", "S SZ O", "S PZ O", "R SZ O", "R PZ O", "S FZ O",
    "S SY O", "QY", "S Y Q", "R SY O", "S SY Q", "R PY1 O", "R Y O", "QZ",
    "S PY2 O", "S PX1 O", "S FY O", "S PY1 Q", "R PX1 O", "R C0 O", "S PX2 O", "S SX O",
    "S Cp O", "S PZ Q", "R Y Q", "R SY Q", "R PY2 O", "S C0 Q", "S SZ Q", "R PY1 Q",
    "S PY3 O", "R FZ O", "S PX1 Q", "S PY2 Q", "S FY Q", "S Cf O", "R PX2 O", "R FY O",
    "S Cs O", "S PX3 O", "R PY3 O", "R SZ Q", "R SX O", "S Cs Q", "R PX1 Q", "S FZ Q",
    "R FY Q", "S PX2 Q", "R PZ Q", "S FX O", "S SX Q", "R FZ Q", "R PY2 Q", "S PY3 Q",
    "S Cf Q", "R SX Q", "S FX Q", "R Cf O", "R PX2 Q", "R FX O", "S PX3 Q", "R C0 Q",
    "S Cp Q", "R PY3 Q", "SIDES", "R FX Q", "R Cf Q", "R PX3 O", "R Cs Q", "R Cs O",
    "R Cp Q", "R Cp O", "R PX3 Q",
)


def gather_kernel(
    p_ref, h_ref, all_ref,
    ss, rs, ds, dr, loc, ins, inr, qs, qr, es, er, xs, xr,
):
    args = (p_ref, h_ref)
    g, d = lax.axis_index("grp"), lax.axis_index("dom")
    x, c = g // 2, g % 2
    z, y = d // 4, d % 4
    odd = x % 2
    u, v = y + odd * (z - y), z + odd * (y - z)
    host = u // 2
    near = {"u": u, "un": u + 1 - 2 * (u % 2)}
    far = v + 1 - 2 * (v % 2)
    ring = {"v": v, "vs": far, "vp": 3 - v, "vf": (3 - v) + 1 - 2 * ((3 - v) % 2)}

    def dom(uu, vv, swap=odd):
        return vv * 4 + uu + swap * 3 * (uu - vv)

    dq = dom(3 - u, v)
    sib_g = g + 1 - 2 * c
    sibling = (sib_g, d)
    aside, back = (g + GROUPS + 2 - 4 * c) % GROUPS, (g + GROUPS - 2 + 4 * c) % GROUPS
    ways = {
        "single": (g, dom(u, far)),
        "pair": (g, dom(u, 3 - v)),
        "cross": (g, dom(near["un"], v)),
        "1": (aside, d),
        "2": (g, dq),
        "3": (back, d),
    }
    is_own = (c + host + 1) % 2
    work_g = is_own * g + (1 - is_own) * sib_g
    work_d = is_own * d + (1 - is_own) * dq

    def worker(to):
        turned = (to // 2) % 2
        across = y + turned * (z - y)
        same = (across // 2 + to + 1) % 2
        there = d + (1 - turned) * (3 - 2 * y) + turned * 4 * (3 - 2 * z)
        return (
            same * to + (1 - same) * (to + 1 - 2 * (to % 2)),
            same * d + (1 - same) * there,
        )

    up_t, down_t = worker((g + 1) % GROUPS), worker((g + GROUPS - 1) % GROUPS)
    partner_idle = (2 * x + host, dq)

    barrier = pltpu.get_barrier_semaphore()
    for who in (
        *ways.values(), sibling, partner_idle,
        ((work_g + GROUPS - 1) % GROUPS, work_d), ((work_g + 1) % GROUPS, work_d),
    ):
        pl.semaphore_signal(barrier, inc=1, device_id=who, device_id_type=MESH)
    pl.semaphore_wait(barrier, 11 - 2 * is_own)

    def at(dom, row, lo, n):
        return all_ref.at[pl.ds((dom * 2 + row) * KEPT + lo, n)]

    def at1(dom, row, lo, n, a):
        return all_ref.at[pl.ds((dom * 2 + row) * KEPT + lo, n), a]

    def remote(src, dst, s, r, who):
        return pltpu.make_async_remote_copy(
            src_ref=src, dst_ref=dst, send_sem=s, recv_sem=r, device_id=who, device_id_type=MESH
        )

    def init_copies(row, to):
        out = []
        for k, (s0, s1, b) in enumerate(PARTS):
            for a in range(2):
                src = args[a].at[row, pl.ds(s0, s1 - s0)]
                dst = at1(d, row, b, s1 - s0, a)
                if to == "own":
                    out.append(pltpu.make_async_copy(src, dst, loc.at[row, k, a]))
                elif to == "sibling":
                    out.append(remote(src, dst, ins.at[row, k, a], inr.at[row, k, a], sibling))
                else:
                    out.append(remote(src, dst, qs.at[row, k, a], qr.at[k, a], (2 * x + row, dq)))
        return out

    def extra_copies(to):
        out = []
        for row in range(2):
            for a in range(2):
                src = args[a].at[row, pl.ds(1, 2)]
                dst = all_ref.at[pl.ds(EXTRA + 2 * row, 2), a]
                if to == "own":
                    out.append(pltpu.make_async_copy(src, dst, es.at[row, a]))
                else:
                    out.append(remote(src, dst, es.at[row, a], er.at[row, a], (sib_g, dq)))
        return out

    def side_copies():
        out = []
        for k, who, parts in ((0, up_t, ((0, 1), (2, 1))), (1, down_t, ((0, 2),))):
            for row in range(2):
                for a in range(2):
                    for q, (first, n) in enumerate(parts):
                        src = args[a].at[row, pl.ds(first, n)]
                        dst = all_ref.at[pl.ds(EXTRA + 4 + 6 * k + 3 * row + first, n), a]
                        out.append(remote(src, dst, xs.at[2 * k + q, row, a], xr.at[2 * k + q, row, a], who))
        return out

    own = c == host
    for core in range(2):

        @pl.when(jnp.logical_and(own, c == core))
        def _():
            mine = init_copies(core, "own")
            theirs = init_copies(1 - core, "sibling")
            for m, t in zip(mine, theirs):
                m.start()
                t.start()
            for copy in init_copies(core, "sibling") + init_copies(1 - core, "own"):
                copy.start()
            for copy in mine:
                copy.wait()

        @pl.when(jnp.logical_and(jnp.logical_not(own), c == core))
        def _():
            for m, t in zip(init_copies(0, "partner"), init_copies(1, "partner")):
                m.start()
                t.start()
            for copy in init_copies(core, "sibling"):
                copy.wait_recv()

    def turn(uu, kind):
        return uu if kind == "O" else 3 - uu

    seen_by = {
        "single": {"v": "vs"},
        "pair": {"v": "vp", "vs": "vf"},
        "cross": {"v": "v", "vs": "vs", "vp": "vp", "vf": "vf"},
    }

    def event(name, kind, side):
        k = NAMES.index(name) + (N_EV if kind == "Q" else 0)
        cut = CUT[kind]
        n = KEPT - cut
        if name in EVENTS:
            part, col, place, way = EVENTS[name]
            if side == "R":
                place = seen_by[way][place]
                if way == "cross":
                    col = "un"
            lo, n = (0, cut) if part == "Z" else (cut, n)
            owner = dom(turn(near[col], kind), ring[place])
            src = dst = at(owner, c, lo, n)
            what = (owner, lo, n, k)
        else:
            way, base = name[2], name[:2]
            col = DETOURS[base]
            what = None
            relay = {h: all_ref.at[pl.ds(RELAY[base + h, kind], n)] for h in "12"}
            if way == "3" and side == "R":
                owner = dom(turn(near[col], kind), 3 - v)
                src = dst = at(owner, c, cut, n)
                what = (owner, cut, n, k)
            elif way == "3":
                owner = dom(turn({"u": v, "un": far}[col], kind), 3 - u, 1 - odd)
                src, dst = relay["2"], at(owner, c, cut, n)
            elif way == "2":
                src, dst = relay["1"], relay["2"]
            else:
                src, dst = at(dom(turn(near[col], kind), v), c, cut, n), relay["1"]
        return remote(src, dst, ss.at[k], rs.at[k], ways[way]), what

    passed = []

    def to_sibling(dom, lo, n, k):
        ref = at(dom, c, lo, n)
        remote(ref, ref, ds.at[k], dr.at[k], sibling).start()
        passed.append((dom, lo, n, k))

    sent = []

    def send(name, kind):
        copy, _ = event(name, kind, "S")
        copy.start()
        sent.append(copy)

    def receive(name, kind):
        copy, what = event(name, kind, "R")
        copy.wait_recv()
        if what is not None:
            to_sibling(*what)

    def receive_partner(parts, lo, n, k):
        for part in parts:
            s0, s1, b = PARTS[part]
            for a in range(2):
                ref = at1(dq, c, b, s1 - s0, a)
                remote(ref, ref, qs.at[0, part, a], qr.at[part, a], sibling).wait_recv()
        to_sibling(dq, lo, n, k)

    sides = side_copies()

    def start_sides():
        for copy in sides:
            copy.start()

        @pl.when(own)
        def _():
            for copy in extra_copies("own"):
                copy.start()

        @pl.when(jnp.logical_not(own))
        def _():
            for copy in extra_copies("partner"):
                copy.start()

    for step in ORDER:
        if step == "SIDES":
            start_sides()
        elif step == "QY":
            receive_partner((0,), CUT["Q"], KEPT - CUT["Q"], 2 * N_EV)
        elif step == "QZ":
            receive_partner((1, 2), 0, CUT["Q"], 2 * N_EV + 1)
        else:
            what, name, kind = step.split()
            (send if what == "S" else receive)(name, kind)

    for core in range(2):

        @pl.when(jnp.logical_and(own, c == core))
        def _():
            for copy in init_copies(1 - core, "own") + extra_copies("own"):
                copy.wait()
            for copy in init_copies(0, "sibling") + init_copies(1, "sibling"):
                copy.wait_send()

        @pl.when(jnp.logical_and(jnp.logical_not(own), c == core))
        def _():
            for copy in init_copies(1 - core, "sibling"):
                copy.wait_recv()
            for copy in init_copies(0, "partner") + init_copies(1, "partner"):
                copy.wait_send()
            for copy in extra_copies("partner"):
                copy.wait()

    for copy in sides:
        copy.wait()
    for copy in sent:
        copy.wait_send()
    for dom, lo, n, k in passed:
        mine, theirs = at(dom, c, lo, n), at(dom, 1 - c, lo, n)
        remote(mine, mine, ds.at[k], dr.at[k], sibling).wait_send()
        remote(theirs, theirs, ds.at[k], dr.at[k], sibling).wait_recv()


def gather(density, hamiltonian):
    dma = pltpu.SemaphoreType.DMA
    return pl.pallas_call(
        gather_kernel,
        name="gather",
        out_shape=jax.ShapeDtypeStruct((LONG, 2, BLK, BLK), jnp.bfloat16),
        in_specs=[pl.BlockSpec(memory_space=pltpu.VMEM)] * 2,
        out_specs=pl.BlockSpec(memory_space=pl.ANY),
        scratch_shapes=[
            dma((2 * N_EV,)), dma((2 * N_EV,)), dma((2 * N_EV + 2,)), dma((2 * N_EV + 2,)),
            dma((2, 3, 2)), dma((2, 3, 2)), dma((2, 3, 2)), dma((2, 3, 2)), dma((3, 2)),
            dma((2, 2)), dma((2, 2)), dma((3, 2, 2)), dma((3, 2, 2)),
        ],
        compiler_params=pltpu.CompilerParams(collective_id=0, has_side_effects=True),
    )(density, hamiltonian)


def row_kernel(
    table, all_ref, x_ref, g_ref, send_ref,
    left, right, low, high, mid, sem_a, sem_b,
):
    def fetch_left(lo, n, at):
        return pltpu.make_async_copy(
            all_ref.at[pl.ds(at, n)], left.at[pl.ds(lo, n)], sem_a.at[lo // KEPT]
        )

    def fetch(e):
        return pltpu.make_async_copy(all_ref.at[table[e]], right.at[e], sem_b.at[e])

    def fetch_step(q, what):
        for k in range(STEP * CHUNK):
            what(fetch(q * (STEP * CHUNK) + k))

    a_copies = (fetch_left(0, KEPT, table[WHERE]), fetch_left(KEPT, 2, table[WHERE + 1]))
    for copy in a_copies:
        copy.start()

    @pl.loop(0, table[WHERE + 2])
    def _(q):
        fetch_step(q, lambda copy: copy.start())

    left[NNZ] = jnp.zeros((2, BLK, BLK), jnp.bfloat16)
    mid[NNZ] = jnp.zeros((2, BLK, BLK), jnp.bfloat16)
    for s in range(NNZ):
        low[s] = jnp.zeros((BLK, 2 * BLK), jnp.float32)
        high[s] = jnp.zeros((BLK, 2 * BLK), jnp.float32)
    for copy in a_copies:
        copy.wait()

    def step(q, a_ref, total):
        sums = []
        for k in range(STEP):
            first = (q * STEP + k) * CHUNK
            e = [first + p for p in range(CHUNK)]
            t = [table[ENTRIES + p] for p in e]
            a = jnp.concatenate([a_ref[p, 0] for p in t], axis=1)
            b = jnp.concatenate([a_ref[p, 1] for p in t], axis=1)
            den = jnp.concatenate([right[p, 0] for p in e], axis=0)
            ham = jnp.concatenate([right[p, 1] for p in e], axis=0)
            both = jnp.dot(a, jnp.concatenate([den, ham], axis=1), preferred_element_type=jnp.float32)
            more = jnp.dot(b, den, preferred_element_type=jnp.float32)
            sums.append((both, more))
        for k in range(STEP):
            s = table[2 * ENTRIES + q * STEP + k]
            both, more = sums[k]
            total[s, :, :BLK] += both[:, :BLK]
            total[s, :, BLK:] += both[:, BLK:] + more

    @pl.loop(0, table[WHERE + 2])
    def _(q):
        fetch_step(q, lambda copy: copy.wait())
        step(q, left, low)

    for s in range(NNZ):
        at = 0 if s == 0 else KEPT - 1 + s if s < 3 else s - 2
        mid[at, 0] = low[s, :, :BLK].astype(jnp.bfloat16)
        mid[at, 1] = low[s, :, BLK:].astype(jnp.bfloat16)

    @pl.loop(0, table[WHERE + 2])
    def _(q):
        step(q, mid, high)

    for s in range(NNZ):
        purified = 3.0 * low[s, :, :BLK] - 2.0 * high[s, :, :BLK]
        gradient = 3.0 * low[s, :, BLK:] - 2.0 * high[s, :, BLK:]
        x_ref[s] = purified
        g_ref[s] = gradient
        send_ref[0, s] = purified.astype(jnp.bfloat16)
        send_ref[1, s] = gradient.astype(jnp.bfloat16)


def one_row(name, table, everything):
    f32, bf16 = jnp.float32, jnp.bfloat16
    vmem = pl.BlockSpec(memory_space=pltpu.VMEM)
    smem = pl.BlockSpec(memory_space=pltpu.SMEM)
    return pl.pallas_call(
        row_kernel,
        name=name,
        out_shape=(
            jax.ShapeDtypeStruct((NNZ, BLK, BLK), f32),
            jax.ShapeDtypeStruct((NNZ, BLK, BLK), f32),
            jax.ShapeDtypeStruct((2, NNZ, BLK, BLK), bf16),
        ),
        in_specs=[smem, pl.BlockSpec(memory_space=pl.ANY)],
        out_specs=(vmem, vmem, vmem),
        scratch_shapes=[
            pltpu.VMEM((NNZ + 1, 2, BLK, BLK), bf16),
            pltpu.VMEM((ENTRIES, 2, BLK, BLK), bf16),
            pltpu.VMEM((NNZ + 1, BLK, 2 * BLK), f32),
            pltpu.VMEM((NNZ + 1, BLK, 2 * BLK), f32),
            pltpu.VMEM((NNZ + 1, 2, BLK, BLK), bf16),
            pltpu.SemaphoreType.DMA((2,)),
            pltpu.SemaphoreType.DMA((ENTRIES,)),
        ],
        compiler_params=pltpu.CompilerParams(vmem_limit_bytes=40 << 20),
        cost_estimate=pl.CostEstimate(
            flops=2 * 2 * 3 * 104 * BLK**3, bytes_accessed=14 << 20, transcendentals=0
        ),
    )(table, everything)


def place_kernel(own, mine_x, mine_g, back, x_in, g_in, x_ref, g_ref, full, sem):
    def store(src, k, q):
        some = pl.ds(4 * q, 4)
        return pltpu.make_async_copy(src.at[some], (x_ref, g_ref)[k].at[1, some], sem.at[k, q])

    parts = [(k, q) for k in range(2) for q in range(4)]

    @pl.when(own[0] == 1)
    def _():
        copies = [store((mine_x, mine_g)[k], k, q) for k, q in parts]
        for copy in copies:
            copy.start()
        for copy in copies:
            copy.wait()

    @pl.when(own[0] == 0)
    def _():
        copies = []
        for k, q in parts:
            full[k, 4 * q : 4 * q + 4] = back[k, 4 * q : 4 * q + 4].astype(jnp.float32)
            copies.append(store(full.at[k], k, q))
            copies[-1].start()
        for copy in copies:
            copy.wait()


def place(own, mine_x, mine_g, back, x, g):
    whole = jax.ShapeDtypeStruct((2, NNZ, BLK, BLK), jnp.float32)
    anywhere, vmem = pl.BlockSpec(memory_space=pl.ANY), pl.BlockSpec(memory_space=pltpu.VMEM)
    return pl.pallas_call(
        place_kernel,
        name="place",
        out_shape=(whole, whole),
        in_specs=[pl.BlockSpec(memory_space=pltpu.SMEM), vmem, vmem, vmem, anywhere, anywhere],
        out_specs=(anywhere, anywhere),
        input_output_aliases={4: 0, 5: 1},
        scratch_shapes=[pltpu.VMEM((2, NNZ, BLK, BLK), jnp.float32), pltpu.SemaphoreType.DMA((2, 4))],
        compiler_params=pltpu.CompilerParams(vmem_limit_bytes=16 << 20),
        cost_estimate=pl.CostEstimate(flops=1 << 20, bytes_accessed=4 << 20, transcendentals=0),
    )(own, mine_x, mine_g, back, x, g)


def tables(pattern, work_g, work_d):
    first = work_g * SPAN + work_d * 2
    cols = lax.dynamic_slice_in_dim(pattern, first, 2, 0)
    picks = (cols.reshape(2 * NNZ, 1) == jnp.arange(pattern.shape[0], dtype=jnp.int32)).astype(jnp.bfloat16)
    far = jnp.dot(picks, pattern.astype(jnp.bfloat16), preferred_element_type=jnp.float32)
    far = far.astype(jnp.int32).reshape(2, NNZ, NNZ)
    slot = jnp.arange(NNZ, dtype=jnp.int32)
    found = jnp.max(
        jnp.where(far[:, :, None, :] == cols[:, None, :, None], slot + 1, 0), axis=3
    ) - 1
    group, inner = cols // SPAN, cols % SPAN
    row = cols % 2
    inside = (group == work_g)[:, :, None]
    before = (group == (work_g + GROUPS - 1) % GROUPS)[:, :, None]
    short = jnp.clip(found, 0, 2)
    place = jnp.where(
        inside,
        jnp.where(
            (found == 1) | (found == 2),
            EXTRA + 2 * row[:, :, None] + jnp.clip(found - 1, 0, 1),
            inner[:, :, None] * KEPT + jnp.where(found < 3, 0, found - 2),
        ),
        EXTRA + 4 + 3 * row[:, :, None] + short + jnp.where(before, 0, 6),
    )
    hit = found >= 0
    held = hit.astype(jnp.int32)
    count = jnp.sum(held, axis=1)
    rank = jnp.sum(jnp.where(slot[None, :, None, None] > slot[None, None, :, None], held[:, None], 0), axis=2)
    chunks = (count + CHUNK - 1) // CHUNK
    start = jnp.sum(jnp.where(slot[None, None, :] < slot[None, :, None], chunks[:, None, :], 0), axis=2)
    spot = jnp.where(hit, start[:, None, :] * CHUNK + rank, -1).reshape(2, 1, NNZ * NNZ)
    chosen = spot == jnp.arange(ENTRIES, dtype=jnp.int32)[None, :, None]
    left_at = jnp.where(slot == 0, 0, jnp.where(slot < 3, KEPT - 1 + slot, slot - 2))
    both = jnp.broadcast_to(left_at[None, :, None] - NNZ, found.shape) + place * 32
    both = jnp.sum(jnp.where(chosen, both.reshape(2, 1, NNZ * NNZ) + NNZ, 0), axis=2)
    slots = jnp.where(jnp.any(chosen, axis=2), both % 32, NNZ)
    places = both // 32
    c = jnp.arange(ENTRIES // CHUNK, dtype=jnp.int32)[None, :, None]
    chunk_s = jnp.sum((c >= (start + chunks)[:, None, :]).astype(jnp.int32), axis=2)
    steps = (jnp.sum(chunks, axis=1, keepdims=True) + STEP - 1) // STEP
    row_at = (work_d * 2 + jnp.arange(2, dtype=jnp.int32)[:, None]) * KEPT
    extra_at = EXTRA + 2 * jnp.arange(2, dtype=jnp.int32)[:, None]
    return jnp.concatenate([places, slots, chunk_s, row_at, extra_at, steps], axis=1)


def on_device(pattern, density, hamiltonian):
    g, d = lax.axis_index("grp"), lax.axis_index("dom")
    odd = g // 2 % 2
    u = jnp.where(odd == 1, d // 4, d % 4)
    own = g % 2 == u // 2
    work_g = jnp.where(own, g, g + 1 - 2 * (g % 2))
    work_d = jnp.where(own, d, d + jnp.where(odd == 1, 4, 1) * (3 - 2 * u))
    lists = tables(pattern, work_g, work_d)
    everything = gather(density, hamiltonian)
    pairs = []
    for gg in range(8):
        for dd in range(16):
            uu, unit = (dd // 4, 4) if gg // 2 % 2 else (dd % 4, 1)
            if gg % 2 != uu // 2:
                pairs.append((gg * 16 + dd, (gg ^ 1) * 16 + dd + unit * (3 - 2 * uu)))
    mine, back = [], []
    for w in range(2):
        px, gx, out = one_row(f"row{w}", lists[w], everything)
        mine.append((px, gx))
        back.append(lax.ppermute(out, ("grp", "dom"), pairs))
    firsts = []
    for k in range(2):
        first = jnp.where(own, mine[0][k], back[0][k].astype(jnp.float32))
        firsts.append(jnp.broadcast_to(first, (2, NNZ, BLK, BLK)))
    return place(own.astype(jnp.int32).reshape(1), *mine[1], back[1], *firsts)


def solution(mesh):
    split = P(("grp", "dom"), None, None, None)
    return jax.shard_map(
        on_device,
        mesh=mesh,
        in_specs=(P(), split, split),
        out_specs=(split, split),
        check_vma=False,
    )
```
